512 devices in a mesh: row: 16 (over z_lo, core), col: 16 (over x, y), dim: 2 (over z_hi).
Axes of the slice: x: 4, y: 4, z: 16 (z_hi: 2, z_lo: 8; z = z_hi * 8 + z_lo), core: 2. Of those that a mesh axis runs over, the one named last changes fastest.
Arguments:
- row_emb: bfloat16 [16, 1024, 256], P('row', None, 'dim'), may hold values from -2 to 2
- col_emb: bfloat16 [16, 1024, 256], P('col', None, 'dim'), may hold values from -2 to 2
- row_acc: float32 [16, 1024], P('row'), may hold values from 0.01 to 1
- col_acc: float32 [16, 1024], P('col'), may hold values from 0.01 to 1
- counts: int32 [16, 16, 1024, 1024], P('row', 'col', 'dim'), may hold values from 0 to 4000, as said below
- live_rows: int32 [16, 16], P('row', 'col'), may hold values from 128 to 1024, as said below
- row_marg: int32 [16, 1024], replicated, may hold values from 1000 to 99999
- col_marg: int32 [16, 1024], replicated, may hold values from 1000 to 99999
Outputs:
- row_new: bfloat16 [16, 1024, 256], P('row', None, 'dim')
- row_acc_new: float32 [16, 1024], P('row')
- col_new: bfloat16 [16, 1024, 256], P('col', None, 'dim')
- col_acc_new: float32 [16, 1024], P('col')
The draws below stay inside these ranges and needn't reach their ends.
Inputs may be any that keep to these rules, and one draw needn't show every extreme that they name: `live_rows`: a multiple of 128; some tile uses all 1024 rows in every draw. About half of the counts are zero.
All inputs are finite; a program needn't handle non-finite values.
Results may differ from the reference program's by a relative error of at most 0.012.
Values may be sent and summed in bfloat16 or wider, within the bound.
No kernel may reach another device: no remote copies, remote signals or barrier semaphores. Data moves between devices by JAX's collectives and lax.ppermute only.
A program may use at most 64 MiB of HBM per device.

```python
import math
import jax
import jax.numpy as jnp
from jax import lax

D = 256
SUB = 1024
STEPS = 2
RBLOCKS = 16
CBLOCKS = 16
N_ROW = 16
N_COL = 16


def draw_counts(key, part):
    key = jax.random.fold_in(key, 11)
    main_key, place_key = jax.random.split(key, 2)
    shape = (N_ROW, N_COL, SUB, SUB)
    source = jax.random.randint(main_key, shape, 0, 2 ** 30)
    present = source % 2
    top_value = source // 2 % 4000
    spread = 1 + source // 8000 % 199
    values = (present * (1 + top_value // spread)).reshape(-1)
    total = N_ROW * N_COL * SUB * SUB
    spot = jax.random.randint(place_key, (), 0, total)
    values = values.at[spot].set(4000)
    return values.reshape(shape).astype(jnp.int32)


def draw_live_rows(key, part):
    key = jax.random.fold_in(key, 23)
    first_key, second_key = jax.random.split(key, 2)
    groups = N_ROW * N_COL
    eighths = jax.random.randint(first_key, (groups,), 1, 9)
    spot = jax.random.randint(second_key, (), 0, groups)
    eighths = jnp.where(jnp.arange(groups) == spot, 8, eighths)
    values = eighths * (SUB // 8)
    return values.reshape(N_ROW, N_COL).astype(jnp.int32)


def touch_ends(values, rng, low, largest):
    index_at = [jax.random.randint(jax.random.fold_in(rng, axis), (), 0, length) for axis, length in enumerate(values.shape)]
    longest = values.shape.index(max(values.shape))
    beside = index_at[:longest] + [(index_at[longest] + 1) % values.shape[longest]] + index_at[longest + 1:]
    return values.at[tuple(index_at)].set(low).at[tuple(beside)].set(largest)


def level_of(rng, dims, cuts, least, largest):
    gain, own = 1.0, jax.random.fold_in(rng, 6)
    for position, shards_of in cuts:
        steps = jnp.exp(jax.random.uniform(jax.random.fold_in(own, position), (shards_of,), jnp.float32, least / len(cuts), largest / len(cuts)))
        gain = gain * jnp.repeat(steps, dims[position] // shards_of).reshape([-1 if axis == position else 1 for axis in range(len(dims))])
    return gain


def normal_values(own_key, shape, deviation, most, pieces=(), kind=jnp.bfloat16):
    values = jax.random.normal(own_key, shape, jnp.float32) * deviation
    if len(pieces) > 0:
        values = level_of(own_key, shape, pieces, -0.22, 0.18) * values
    return jnp.clip(values, min=-most, max=most).astype(kind)


def setup_inputs(seed: int = 0) -> dict:
    keys = jax.random.split(jax.random.key(seed), 9)
    row_emb = normal_values(keys[0], (RBLOCKS, SUB, D), 0.35, 2.0, ((0, 16), (2, 2)))
    col_emb = normal_values(keys[1], (CBLOCKS, SUB, D), 0.35, 2.0, ((0, 16), (2, 2)))
    row_acc = jnp.clip(jnp.exp(math.log(1.0) - 4.6051702 * jax.random.uniform(keys[2], (RBLOCKS, SUB), jnp.float32) ** level_of(keys[2], (RBLOCKS, SUB), ((0, 16),), -0.2, 0.2)), 0.01, 1.0)
    col_acc = jnp.clip(jnp.exp(math.log(1.0) - 4.6051702 * jax.random.uniform(keys[3], (CBLOCKS, SUB), jnp.float32) ** level_of(keys[3], (CBLOCKS, SUB), ((0, 16),), -0.2, 0.2)), 0.01, 1.0)
    counts = draw_counts(jax.random.fold_in(keys[8], 71), 0)
    live_rows = draw_live_rows(jax.random.fold_in(keys[8], 71), 0)
    row_marg = touch_ends(jax.random.randint(keys[6], (RBLOCKS, SUB), 1000, 100000), jax.random.fold_in(keys[6], 1), 1000, 99999).astype(jnp.int32)
    col_marg = touch_ends(jax.random.randint(keys[7], (CBLOCKS, SUB), 1000, 100000), jax.random.fold_in(keys[7], 1), 1000, 99999).astype(jnp.int32)
    return dict(row_emb=row_emb, col_emb=col_emb, row_acc=row_acc, col_acc=col_acc, counts=counts, live_rows=live_rows, row_marg=row_marg, col_marg=col_marg)


learn_rate = 0.1

def cell_grad(scores, tile_counts, shift_log):
    count_f = tile_counts.astype(jnp.float32)
    target = jnp.log(jnp.maximum(count_f, 1.0)) + shift_log
    confidence = 0.1 + 0.25 * jnp.sqrt(count_f)
    return jnp.where(tile_counts > 0, confidence * (scores - target), jax.nn.sigmoid(scores - shift_log))

def reference(row_emb, col_emb, row_acc, col_acc, counts, live_rows, row_marg, col_marg):
    half_d = D // 2
    contract_last = (((1,), (1,)), ((), ()))
    contract_first = (((0,), (0,)), ((), ()))
    log_total = jnp.log(jnp.sum(row_marg).astype(jnp.float32))
    log_rows = jnp.log(row_marg.astype(jnp.float32))
    log_cols = jnp.log(col_marg.astype(jnp.float32))
    row_index = jnp.arange(SUB, dtype=jnp.int32)

    def one_step(emb_rows, emb_cols):

        def group(gradients, group_idx):
            row_grad, col_grad = gradients
            row_grid = group_idx // N_COL
            col_grid = group_idx % N_COL
            w_block = emb_rows[row_grid]
            c_block = emb_cols[col_grid]
            lower_half = lax.dot_general(w_block[:, :half_d], c_block[:, :half_d], contract_last, preferred_element_type=jnp.float32).astype(jnp.bfloat16)
            upper_half = lax.dot_general(w_block[:, half_d:], c_block[:, half_d:], contract_last, preferred_element_type=jnp.float32).astype(jnp.bfloat16)
            scores = lower_half.astype(jnp.float32) + upper_half.astype(jnp.float32)
            shift_log = log_total - log_rows[row_grid][:, None] - log_cols[col_grid][None, :]
            grad_tile = cell_grad(scores, counts[row_grid, col_grid], shift_log) / SUB
            live_mask = row_index < live_rows[row_grid, col_grid]
            grad_tile = jnp.where(live_mask[:, None], grad_tile, 0.0).astype(jnp.bfloat16)
            row_term = jnp.dot(grad_tile, c_block, preferred_element_type=jnp.float32)
            col_term = lax.dot_general(grad_tile, w_block, contract_first, preferred_element_type=jnp.float32)
            row_grad = row_grad.at[row_grid].add(row_term)
            col_grad = col_grad.at[col_grid].add(col_term)
            return ((row_grad, col_grad), None)
        initial = (jnp.zeros((RBLOCKS, SUB, D), jnp.float32), jnp.zeros((CBLOCKS, SUB, D), jnp.float32))
        result, unused = lax.scan(group, initial, jnp.arange(N_ROW * N_COL, dtype=jnp.int32))
        return result
    emb_rows, emb_cols, acc_rows, acc_cols = (row_emb, col_emb, row_acc, col_acc)
    for step in range(STEPS):
        row_grad, col_grad = one_step(emb_rows, emb_cols)
        acc_rows = acc_rows + lax.optimization_barrier(jnp.sum(row_grad * row_grad, axis=2)) / D
        acc_cols = acc_cols + lax.optimization_barrier(jnp.sum(col_grad * col_grad, axis=2)) / D
        emb_rows = (emb_rows.astype(jnp.float32) - learn_rate * row_grad / jnp.sqrt(acc_rows)[:, :, None]).astype(jnp.bfloat16)
        emb_cols = (emb_cols.astype(jnp.float32) - learn_rate * col_grad / jnp.sqrt(acc_cols)[:, :, None]).astype(jnp.bfloat16)
    return (emb_rows, acc_rows, emb_cols, acc_cols)
```

```python
import jax
import jax.numpy as jnp
from jax import lax
from jax.sharding import PartitionSpec as P

STEPS = 2
LEARN_RATE = 0.1
SIDE = 1024
HALF_ROWS = 512
WIDTH = 256
HALF_D = 128
N_COL = 16
ROW_PART = HALF_ROWS // N_COL
COL_PART = 128

CORE_PAIRS = [[2 * z, 2 * z + 1] for z in range(8)]
Z_QUADS = [[2 * (4 * h + k) + core for k in range(4)] for h in range(2) for core in range(2)]
FAR_Z = [(i, i ^ 8) for i in range(16)]
DIM_SWAP = [(0, 1), (1, 0)]


def swap_halves(block):
    return jnp.concatenate([block[:, HALF_D:], block[:, :HALF_D]], axis=1)


def adagrad(total, acc, emb):
    squares = total * total
    square = jnp.sum(squares[:, :HALF_D] + squares[:, HALF_D:], axis=1, keepdims=True)
    acc = acc + square / WIDTH
    emb = emb.astype(jnp.float32) - LEARN_RATE * total / jnp.sqrt(acc)
    return emb.astype(jnp.bfloat16), acc


def spread(block, count):
    return jnp.broadcast_to(block[None], (count,) + block.shape)


def split(values):
    high = lax.reduce_precision(values, 8, 7)
    return high.astype(jnp.bfloat16), (values - high).astype(jnp.bfloat16)


def joined(parts):
    high, low = parts
    return high.astype(jnp.float32) + low.astype(jnp.float32)


def with_acc(emb, acc):
    flat = jnp.concatenate(split(acc[:, 0]))
    width = emb.shape[1]
    flat = jnp.pad(flat, (0, 8 * width - flat.shape[0])).reshape(8, width)
    return jnp.concatenate([emb, flat])


def without_acc(blocks, count):
    k, _, width = blocks.shape
    flat = blocks[:, count:].reshape(k, 8 * width)
    parts = flat[:, :count].reshape(-1), flat[:, count : 2 * count].reshape(-1)
    return blocks[:, :count].reshape(k * count, width), parts


def shards(row_emb, col_emb, row_acc, col_acc, counts, live_rows, row_marg, col_marg):
    d, r, c = (lax.axis_index(a) for a in ("dim", "row", "col"))
    core, quad = r % 2, (r // 2) % 4
    row_emb, col_emb = row_emb[0], col_emb[0]

    def rows_at(block, start, size):
        return lax.dynamic_slice_in_dim(block, start, size, 0)

    col_at = core * HALF_ROWS + quad * COL_PART
    row_at = d * HALF_ROWS + c * ROW_PART

    sent = jnp.concatenate(
        [rows_at(row_emb, (1 - d) * HALF_ROWS, HALF_ROWS), rows_at(col_emb, core * HALF_ROWS, HALF_ROWS)]
    )
    got = lax.ppermute(sent, "dim", DIM_SWAP)
    col_other = lax.all_gather(got[HALF_ROWS:], "row", tiled=True, axis_index_groups=CORE_PAIRS)
    rows = jnp.concatenate([rows_at(row_emb, d * HALF_ROWS, HALF_ROWS), got[:HALF_ROWS]], axis=1)
    cols = jnp.concatenate([col_emb, col_other], axis=1)

    log_total = jnp.log(jnp.sum(row_marg).astype(jnp.float32))
    own_marg = lax.dynamic_index_in_dim(row_marg, r, 0, False)
    row_logs = jnp.log(rows_at(own_marg, d * HALF_ROWS, HALF_ROWS).astype(jnp.float32))
    col_logs = jnp.log(lax.dynamic_index_in_dim(col_marg, c, 0, False).astype(jnp.float32))
    shift_log = log_total - row_logs[:, None] - col_logs[None, :]
    tile = counts[0, 0]
    count_f = tile.astype(jnp.float32)
    present = tile > 0
    live = d * HALF_ROWS + jnp.arange(HALF_ROWS, dtype=jnp.int32) < live_rows[0, 0]
    weight = jnp.where(present, (0.1 + 0.25 * jnp.sqrt(count_f)) / SIDE, 0.0)
    target = jnp.log(jnp.maximum(count_f, 1.0)) + shift_log
    weight, target = lax.optimization_barrier((weight, target))

    row_acc = rows_at(row_acc[0], row_at, ROW_PART)[:, None]
    col_acc = rows_at(col_acc[0], col_at, COL_PART)[:, None]

    for step in range(STEPS):
        last = step == STEPS - 1
        scores = lax.dot_general(
            rows, cols, (((1,), (1,)), ((), ())), preferred_element_type=jnp.float32
        )
        gap = scores - target
        cell = jnp.where(weight > 0, weight * gap, jax.nn.sigmoid(gap) / SIDE)
        grad = jnp.where(live[:, None], cell, 0.0).astype(jnp.bfloat16)
        row_term = jnp.dot(grad, cols, preferred_element_type=jnp.float32).astype(jnp.bfloat16)
        col_term = lax.dot_general(
            grad, rows, (((0,), (0,)), ((), ())), preferred_element_type=jnp.float32
        ).astype(jnp.bfloat16)

        kept = rows_at(col_term, core * HALF_ROWS, HALF_ROWS)
        given = rows_at(col_term, (1 - core) * HALF_ROWS, HALF_ROWS)
        pair = lax.all_gather(given, "row", axis_index_groups=CORE_PAIRS)
        taken = lax.dynamic_index_in_dim(pair, 1 - core, 0, False)
        half = (kept.astype(jnp.float32) + taken.astype(jnp.float32)).astype(jnp.bfloat16)
        parts = lax.all_to_all(
            half.reshape(4, COL_PART, WIDTH), "row", 0, 0, axis_index_groups=Z_QUADS
        )
        near = jnp.sum(parts.astype(jnp.float32), axis=0).astype(jnp.bfloat16)
        far = lax.ppermute(near, "row", FAR_Z)

        row_parts = lax.all_to_all(row_term.reshape(N_COL, ROW_PART, WIDTH), "col", 0, 0)
        row_parts, far = lax.optimization_barrier((row_parts, far))

        near = (near.astype(jnp.float32) + far.astype(jnp.float32)).astype(jnp.bfloat16)
        far = lax.ppermute(near, "dim", DIM_SWAP)
        row_total = jnp.sum(row_parts.astype(jnp.float32), axis=0)
        row_new, row_acc = adagrad(row_total, row_acc, rows_at(rows, c * ROW_PART, ROW_PART))
        if last:
            row_new = with_acc(row_new, row_acc)
        rows = lax.all_to_all(spread(row_new, N_COL), "col", 0, 0)
        if last:
            rows, acc_rows = without_acc(rows, ROW_PART)
            rows_far = jnp.concatenate([rows[:, HALF_D:], jnp.concatenate(acc_rows).reshape(8, HALF_D)])
            rows_far = lax.ppermute(rows_far, "dim", DIM_SWAP)
            flat = rows_far[HALF_ROWS:].reshape(-1)
            rows_far, acc_rows_far = rows_far[:HALF_ROWS], (flat[:HALF_ROWS], flat[HALF_ROWS:])
        else:
            rows = rows.reshape(HALF_ROWS, WIDTH)
        col_total = near.astype(jnp.float32) + swap_halves(far).astype(jnp.float32)
        col_new, col_acc = adagrad(col_total, col_acc, rows_at(cols, col_at, COL_PART))
        if last:
            col_new = with_acc(col_new[:, :HALF_D], col_acc)
        quarter = lax.all_to_all(spread(col_new, 4), "row", 0, 0, axis_index_groups=Z_QUADS)
        cols = lax.all_gather(quarter, "row", tiled=True, axis_index_groups=CORE_PAIRS)
        if last:
            cols, acc_cols = without_acc(cols, COL_PART)
        else:
            cols = cols.reshape(SIDE, WIDTH)

    own = rows[:, :HALF_D]
    row_out = jnp.where(
        d == 0, jnp.concatenate([own, rows_far]), jnp.concatenate([rows_far, own])
    )
    acc_own, acc_far = joined(acc_rows), joined(acc_rows_far)
    row_acc_out = jnp.where(
        d == 0, jnp.concatenate([acc_own, acc_far]), jnp.concatenate([acc_far, acc_own])
    )
    return row_out[None], row_acc_out[None], cols[None], joined(acc_cols)[None]


def solution(mesh):
    return jax.shard_map(
        shards,
        mesh=mesh,
        in_specs=(
            P("row", None, "dim"),
            P("col", None, "dim"),
            P("row", None),
            P("col", None),
            P("row", "col", "dim", None),
            P("row", "col"),
            P(),
            P(),
        ),
        out_specs=(P("row", None, "dim"), P("row", None), P("col", None, "dim"), P("col", None)),
        check_vma=False,
    )
```

```python
import jax
import jax.numpy as jnp
from jax import lax
from jax.experimental import pallas as pl
from jax.experimental.pallas import tpu as pltpu
from jax.sharding import PartitionSpec as P

STEPS = 2
LEARN_RATE = 0.1
SIDE = 1024
HALF_ROWS = 512
WIDTH = 256
HALF_D = 128
N_COL = 16
ROW_PART = HALF_ROWS // N_COL
COL_PART = 128
FAR_ROWS = COL_PART + ROW_PART

C_PAIR, C_ROW, C_COL = 20, 1, 20

CORE_PAIRS = [[2 * z, 2 * z + 1] for z in range(8)]
Z_QUADS = [[2 * (4 * h + k) + core for k in range(4)] for h in range(2) for core in range(2)]
FAR_Z = [(i, i ^ 8) for i in range(16)]
DIM_SWAP = [(0, 1), (1, 0)]


def swap_halves(block):
    return jnp.concatenate([block[:, HALF_D:], block[:, :HALF_D]], axis=1)


def adagrad(total, acc, emb):
    squares = total * total
    square = jnp.sum(squares[:, :HALF_D] + squares[:, HALF_D:], axis=1, keepdims=True)
    acc = acc + square / WIDTH
    emb = emb.astype(jnp.float32) - LEARN_RATE * total / jnp.sqrt(acc)
    return emb.astype(jnp.bfloat16), acc


def acc_lanes(acc, start, width):
    high = acc.astype(jnp.bfloat16).astype(jnp.float32)
    lane = lax.broadcasted_iota(jnp.int32, (acc.shape[0], HALF_D), 1) - start
    part = jnp.where(lane < width, high, acc - high)
    return jnp.where((lane >= 0) & (lane < 2 * width), part, 0.0).astype(jnp.bfloat16)


def pair_kernel(part, mine, theirs, both):
    both[...] = (mine[...].astype(jnp.float32) + theirs[...].astype(jnp.float32)).astype(jnp.bfloat16)


def row_kernel(part, parts, acc, emb, emb_out, acc_out):
    total = jnp.sum(parts[...].astype(jnp.float32), axis=0)
    emb_new, acc_out[...] = adagrad(total, acc[...], emb[0])
    emb_out[...] = jnp.broadcast_to(emb_new[None], emb_out.shape)


def row_last_kernel(part, parts, acc, emb, near, kept, sent):
    total = jnp.sum(parts[...].astype(jnp.float32), axis=0)
    emb_new, acc_new = adagrad(total, acc[...], emb[0])
    kept[:, :HALF_D] = emb_new[:, :HALF_D]
    kept[:, HALF_D:] = acc_lanes(acc_new, 0, 32)
    sent[:COL_PART, :] = near[...]
    sent[COL_PART:, :HALF_D] = emb_new[:, HALF_D:]
    sent[COL_PART:, HALF_D:] = acc_lanes(acc_new, 64, 32)


def col_kernel(part, mine, theirs, acc, emb, emb_out, acc_out):
    total = mine[...].astype(jnp.float32) + swap_halves(theirs[...].astype(jnp.float32))
    emb_new, acc_out[...] = adagrad(total, acc[...], emb[0])
    emb_out[...] = jnp.broadcast_to(emb_new[None], emb_out.shape)


def col_last_kernel(part, mine, theirs, acc, emb, kept, col_out, row_out):
    total = mine[...].astype(jnp.float32) + swap_halves(theirs[:COL_PART, :].astype(jnp.float32))
    emb_new, acc_new = adagrad(total, acc[...], emb[0])
    col_new = jnp.concatenate([emb_new[:, :HALF_D], acc_lanes(acc_new, 0, 64)], axis=1)
    col_out[...] = jnp.broadcast_to(col_new[None], col_out.shape)
    there = theirs[COL_PART:, :]
    here = kept[...]
    both = (here[:, HALF_D:].astype(jnp.float32) + there[:, HALF_D:].astype(jnp.float32)).astype(jnp.bfloat16)
    row_new = jnp.concatenate([here[:, :HALF_D], there[:, :HALF_D], both], axis=1)
    row_out[...] = jnp.broadcast_to(row_new[None], row_out.shape)


def on_device(kernel, part, operands, shapes, micros, chunk=None):
    def whole(shape):
        zeros = (0,) * len(shape)
        return pl.BlockSpec(shape, lambda i, s: zeros)

    def one(shape):
        rest = (0,) * (len(shape) - 1)
        return pl.BlockSpec((1,) + shape[1:], lambda i, s: (s[0],) + rest)

    return pl.pallas_call(
        kernel,
        grid_spec=pltpu.PrefetchScalarGridSpec(
            num_scalar_prefetch=1,
            grid=(1,),
            in_specs=[one(o.shape) if k == chunk else whole(o.shape) for k, o in enumerate(operands)],
            out_specs=[whole(o.shape) for o in shapes],
        ),
        out_shape=shapes,
        cost_estimate=pl.CostEstimate(flops=micros * 10**9, bytes_accessed=1 << 20, transcendentals=0),
    )(part, *operands)


def bf16(*shape):
    return jax.ShapeDtypeStruct(shape, jnp.bfloat16)


def f32(*shape):
    return jax.ShapeDtypeStruct(shape, jnp.float32)


def spread(block, count):
    return jnp.broadcast_to(block[None], (count,) + block.shape)


def joined(block, high, low):
    return (block[:, :, high].astype(jnp.float32) + block[:, :, low].astype(jnp.float32)).reshape(-1)


def shards(row_emb, col_emb, row_acc, col_acc, counts, live_rows, row_marg, col_marg):
    d, r, c = (lax.axis_index(a) for a in ("dim", "row", "col"))
    core, quad = r % 2, (r // 2) % 4
    row_emb, col_emb = row_emb[0], col_emb[0]
    col_part = core * 4 + quad

    def rows_at(block, start, size):
        return lax.dynamic_slice_in_dim(block, start, size, 0)

    col_got = lax.ppermute(rows_at(col_emb, col_part * COL_PART, COL_PART), "dim", DIM_SWAP)
    row_got = lax.ppermute(rows_at(row_emb, (1 - d) * HALF_ROWS, HALF_ROWS), "dim", DIM_SWAP)
    col_other = lax.all_to_all(spread(col_got, 4), "row", 0, 0, axis_index_groups=Z_QUADS)
    col_other = lax.all_gather(col_other, "row", tiled=True, axis_index_groups=CORE_PAIRS)
    rows = jnp.concatenate([rows_at(row_emb, d * HALF_ROWS, HALF_ROWS), row_got], axis=1)
    cols = jnp.concatenate([col_emb, col_other.reshape(SIDE, HALF_D)], axis=1)

    log_total = jnp.log(jnp.sum(row_marg).astype(jnp.float32))
    own_marg = lax.dynamic_index_in_dim(row_marg, r, 0, False)
    row_logs = jnp.log(rows_at(own_marg, d * HALF_ROWS, HALF_ROWS).astype(jnp.float32))
    col_logs = jnp.log(lax.dynamic_index_in_dim(col_marg, c, 0, False).astype(jnp.float32))
    shift_log = log_total - row_logs[:, None] - col_logs[None, :]
    tile = counts[0, 0]
    count_f = tile.astype(jnp.float32)
    present = tile > 0
    live = d * HALF_ROWS + jnp.arange(HALF_ROWS, dtype=jnp.int32) < live_rows[0, 0]
    weight = jnp.where(present, (0.1 + 0.25 * jnp.sqrt(count_f)) / SIDE, 0.0)
    target = jnp.log(jnp.maximum(count_f, 1.0)) + shift_log
    row_acc = rows_at(row_acc[0], d * HALF_ROWS + c * ROW_PART, ROW_PART)[:, None]
    col_acc = rows_at(col_acc[0], col_part * COL_PART, COL_PART)[:, None]
    row_at, col_at = c.reshape(1).astype(jnp.int32), col_part.reshape(1).astype(jnp.int32)
    weight, target, row_acc, col_acc, row_at, col_at = lax.optimization_barrier(
        (weight, target, row_acc, col_acc, row_at, col_at)
    )

    for step in range(STEPS):
        last = step == STEPS - 1
        scores = lax.dot_general(
            rows, cols, (((1,), (1,)), ((), ())), preferred_element_type=jnp.float32
        )
        gap = scores - target
        cell = jnp.where(weight > 0, weight * gap, jax.nn.sigmoid(gap) / SIDE)
        grad = jnp.where(live[:, None], cell, 0.0).astype(jnp.bfloat16)
        col_term = lax.dot_general(
            grad, rows, (((0,), (0,)), ((), ())), preferred_element_type=jnp.float32
        ).astype(jnp.bfloat16)

        kept = rows_at(col_term, core * HALF_ROWS, HALF_ROWS)
        given = rows_at(col_term, (1 - core) * HALF_ROWS, HALF_ROWS)
        pair = lax.all_gather(given, "row", axis_index_groups=CORE_PAIRS)
        taken = lax.dynamic_index_in_dim(pair, 1 - core, 0, False)
        half = (kept.astype(jnp.float32) + taken.astype(jnp.float32)).astype(jnp.bfloat16)
        parts = lax.all_to_all(
            half.reshape(4, COL_PART, WIDTH), "row", 0, 0, axis_index_groups=Z_QUADS
        )
        near = jnp.sum(parts.astype(jnp.float32), axis=0).astype(jnp.bfloat16)
        grad, near = lax.optimization_barrier((grad, near))
        far = lax.ppermute(near, "row", FAR_Z)

        row_term = jnp.dot(grad, cols, preferred_element_type=jnp.float32).astype(jnp.bfloat16)
        row_parts = lax.all_to_all(row_term.reshape(N_COL, ROW_PART, WIDTH), "col", 0, 0)
        (near,) = on_device(pair_kernel, row_at, (near, far), (bf16(COL_PART, WIDTH),), C_PAIR)
        rows = rows.reshape(N_COL, ROW_PART, WIDTH)
        cols = cols.reshape(8, COL_PART, WIDTH)
        if not last:
            far = lax.ppermute(near, "dim", DIM_SWAP)
            rows, row_acc = on_device(
                row_kernel,
                row_at,
                (row_parts, row_acc, rows),
                (bf16(N_COL, ROW_PART, WIDTH), f32(ROW_PART, 1)),
                C_ROW,
                2,
            )
            rows = lax.all_to_all(rows, "col", 0, 0).reshape(HALF_ROWS, WIDTH)
            cols, col_acc = on_device(
                col_kernel,
                col_at,
                (near, far, col_acc, cols),
                (bf16(4, COL_PART, WIDTH), f32(COL_PART, 1)),
                C_COL,
                3,
            )
            rows, cols = lax.optimization_barrier((rows, cols))
            cols = lax.all_to_all(cols, "row", 0, 0, axis_index_groups=Z_QUADS)
            cols = lax.all_gather(cols, "row", tiled=True, axis_index_groups=CORE_PAIRS)
            cols = cols.reshape(SIDE, WIDTH)
            continue

        kept, sent = on_device(
            row_last_kernel,
            row_at,
            (row_parts, row_acc, rows, near),
            (bf16(ROW_PART, WIDTH), bf16(FAR_ROWS, WIDTH)),
            1,
            2,
        )
        far = lax.ppermute(sent, "dim", DIM_SWAP)
        cols, rows = on_device(
            col_last_kernel,
            col_at,
            (near, far, col_acc, cols, kept),
            (bf16(4, COL_PART, WIDTH), bf16(N_COL, ROW_PART, WIDTH + HALF_D)),
            1,
            3,
        )
        cols = lax.all_to_all(cols, "row", 0, 0, axis_index_groups=Z_QUADS)
        rows, cols = lax.optimization_barrier((rows, cols))
        rows = lax.all_to_all(rows, "col", 0, 0)
        cols = lax.all_gather(cols, "row", tiled=True, axis_index_groups=CORE_PAIRS)
        rows, cols = lax.optimization_barrier((rows, cols))
    here = rows[:, :, :HALF_D].reshape(HALF_ROWS, HALF_D)
    there = rows[:, :, HALF_D:WIDTH].reshape(HALF_ROWS, HALF_D)
    row_out = jnp.where(d == 0, jnp.concatenate([here, there]), jnp.concatenate([there, here]))
    here = joined(rows, WIDTH, WIDTH + 32)
    there = joined(rows, WIDTH + 64, WIDTH + 96)
    row_acc_out = jnp.where(d == 0, jnp.concatenate([here, there]), jnp.concatenate([there, here]))
    col_out = cols[:, :, :HALF_D].reshape(SIDE, HALF_D)
    col_acc_out = joined(cols, HALF_D, HALF_D + 64)
    return row_out[None], row_acc_out[None], col_out[None], col_acc_out[None]


def solution(mesh):
    return jax.shard_map(
        shards,
        mesh=mesh,
        in_specs=(
            P("row", None, "dim"),
            P("col", None, "dim"),
            P("row", None),
            P("col", None),
            P("row", "col", "dim", None),
            P("row", "col"),
            P(),
            P(),
        ),
        out_specs=(P("row", None, "dim"), P("row", None), P("col", None, "dim"), P("col", None)),
        check_vma=False,
    )
```

```python
import jax
import jax.numpy as jnp
from jax import lax
from jax.experimental import pallas as pl
from jax.experimental.pallas import tpu as pltpu
from jax.sharding import PartitionSpec as P

STEPS = 2
LEARN_RATE = 0.1
SIDE = 1024
HALF_ROWS = 512
WIDTH = 256
HALF_D = 128
N_COL = 16
ROW_PART = HALF_ROWS // N_COL
COL_PART = 128
ROW_PAIR = 256
TILE_ROWS = 256

C_SHARE, C_PAIR, C_ROW, C_COL, C_ROW_LAST, C_COL_LAST, C_PACK = 20, 20, 1, 20, 1, 20, 20

CORE_PAIRS = [[2 * z, 2 * z + 1] for z in range(8)]
Z_QUADS = [[2 * (4 * h + k) + core for k in range(4)] for h in range(2) for core in range(2)]
FAR_Z = [(i, i ^ 8) for i in range(16)]
Y_SWAP = [(i, i ^ 1) for i in range(16)]
DIM_SWAP = [(0, 1), (1, 0)]

AT_DIM, AT_COL, AT_CORE, AT_COL_PART, AT_Y, AT_LIVE = range(6)


def to_f32(block):
    return block.astype(jnp.float32)


def swap_halves(block):
    return jnp.concatenate([block[:, HALF_D:], block[:, :HALF_D]], axis=1)


def diagonal(n):
    return lax.broadcasted_iota(jnp.int32, (n, n), 0) == lax.broadcasted_iota(jnp.int32, (n, n), 1)


def column(acc):
    if acc.shape[0] > 1:
        return acc
    return jnp.sum(jnp.where(diagonal(acc.shape[1]), acc, 0.0), axis=1, keepdims=True)


def line(acc):
    return jnp.sum(jnp.where(diagonal(acc.shape[0]), acc, 0.0), axis=0, keepdims=True)


def adagrad(total, acc, emb):
    squares = total * total
    square = jnp.sum(squares[:, :HALF_D] + squares[:, HALF_D:], axis=1, keepdims=True)
    acc = acc + square / WIDTH
    emb = to_f32(emb) - LEARN_RATE * total / jnp.sqrt(acc)
    return emb.astype(jnp.bfloat16), acc


def acc_lanes(acc, start, width):
    high = to_f32(acc.astype(jnp.bfloat16))
    lane = lax.broadcasted_iota(jnp.int32, (acc.shape[0], HALF_D), 1) - start
    part = jnp.where(lane < width, high, acc - high)
    return jnp.where((lane >= 0) & (lane < 2 * width), part, 0.0).astype(jnp.bfloat16)


def block_at(ref, index, size):
    return ref[pl.ds(pl.multiple_of(index * size, size), size), :]


def share_kernel(at, got, out):
    out[...] = jnp.broadcast_to(got[:COL_PART, :][None], out.shape)


def tile_terms(at, rows, cols, weight, target, kept, given, row_term, col_sum):
    cols_all = cols[...]
    for part in range(HALF_ROWS // TILE_ROWS):
        here = slice(part * TILE_ROWS, (part + 1) * TILE_ROWS)
        rows_here = rows[here, :]
        scores = lax.dot_general(
            rows_here, cols_all, (((1,), (1,)), ((), ())), preferred_element_type=jnp.float32
        )
        gap = scores - target[here, :]
        scale = weight[here, :]
        sigmoid = (0.5 / SIDE) * jnp.tanh(0.5 * gap) + 0.5 / SIDE
        cell = jnp.where(scale > 0, scale * gap, sigmoid)
        row = lax.broadcasted_iota(jnp.int32, cell.shape, 0) + part * TILE_ROWS
        grad = jnp.where(row < at[AT_LIVE], cell, 0.0).astype(jnp.bfloat16)
        row_term[here, :] = jnp.dot(grad, cols_all, preferred_element_type=jnp.float32).astype(jnp.bfloat16)
        term = lax.dot_general(
            grad, rows_here, (((0,), (0,)), ((), ())), preferred_element_type=jnp.float32
        )
        if part == 0:
            col_sum[...] = term
        else:
            col_sum[...] += term
    core = at[AT_CORE]
    kept[...] = block_at(col_sum, core, HALF_ROWS).astype(jnp.bfloat16)
    given[...] = block_at(col_sum, 1 - core, HALF_ROWS).astype(jnp.bfloat16)


def first_tile_kernel(
    at, row_emb, got, there, col_emb, col_other, weight, target, kept, given, row_term, rows, cols, col_sum
):
    side, y = at[AT_DIM], at[AT_Y]
    rows[:, :HALF_D] = block_at(row_emb, side, HALF_ROWS)
    rows[pl.ds(pl.multiple_of(y * ROW_PAIR, ROW_PAIR), ROW_PAIR), HALF_D:] = got[COL_PART:, :]
    rows[pl.ds(pl.multiple_of((1 - y) * ROW_PAIR, ROW_PAIR), ROW_PAIR), HALF_D:] = there[...]
    cols[:, :HALF_D] = col_emb[...]
    cols[:, HALF_D:] = col_other[...]
    tile_terms(at, rows, cols, weight, target, kept, given, row_term, col_sum)


def same_kernel(at, block, out):
    out[...] = block[...]


def half_kernel(at, kept, pair, half):
    theirs = pair[pl.ds(1 - at[AT_CORE], 1), :, :][0]
    half[...] = (to_f32(kept[...]) + to_f32(theirs)).astype(jnp.bfloat16).reshape(half.shape)


def near_kernel(at, parts, near):
    near[...] = jnp.sum(to_f32(parts[...]), axis=0).astype(jnp.bfloat16)


def pair_kernel(at, mine, theirs, both):
    both[...] = (to_f32(mine[...]) + to_f32(theirs[...])).astype(jnp.bfloat16)


def row_kernel(at, parts, acc, rows, emb_out, acc_out):
    total = jnp.sum(to_f32(parts[...]), axis=0)
    emb_new, acc_out[...] = adagrad(total, column(acc[...]), block_at(rows, at[AT_COL], ROW_PART))
    emb_out[...] = jnp.broadcast_to(emb_new[None], emb_out.shape)


def row_last_kernel(at, parts, acc, rows, kept, sent):
    total = jnp.sum(to_f32(parts[...]), axis=0)
    emb_new, acc_new = adagrad(total, acc[...], block_at(rows, at[AT_COL], ROW_PART))
    kept[:, :HALF_D] = emb_new[:, :HALF_D]
    kept[:, HALF_D:] = acc_lanes(acc_new, 0, 32)
    sent[:, :HALF_D] = emb_new[:, HALF_D:]
    sent[:, HALF_D:] = acc_lanes(acc_new, 64, 32)


def col_kernel(at, mine, theirs, acc, cols, emb_out, acc_out):
    total = to_f32(mine[...]) + swap_halves(to_f32(theirs[...]))
    emb_new, acc_out[...] = adagrad(total, column(acc[...]), block_at(cols, at[AT_COL_PART], COL_PART))
    emb_out[...] = jnp.broadcast_to(emb_new[None], emb_out.shape)


def col_last_kernel(at, mine, theirs, acc, cols, col_out):
    total = to_f32(mine[...]) + swap_halves(to_f32(theirs[...]))
    emb_new, acc_new = adagrad(total, acc[...], block_at(cols, at[AT_COL_PART], COL_PART))
    col_new = jnp.concatenate([emb_new[:, :HALF_D], acc_lanes(acc_new, 0, 64)], axis=1)
    col_out[...] = jnp.broadcast_to(col_new[None], col_out.shape)


def pack_kernel(at, kept, theirs, row_out):
    here, there = kept[...], theirs[...]
    both = (to_f32(here[:, HALF_D:]) + to_f32(there[:, HALF_D:])).astype(jnp.bfloat16)
    row_new = jnp.concatenate([here[:, :HALF_D], there[:, :HALF_D], both], axis=1)
    row_out[...] = jnp.broadcast_to(row_new[None], row_out.shape)


def out_kernel(at, rows, cols, row_out, row_acc_out, col_out, col_acc_out):
    side = at[AT_DIM]
    for half, first in ((side, 0), (1 - side, HALF_D)):
        start = pl.multiple_of(half * HALF_ROWS, HALF_ROWS)
        row_out[0, pl.ds(start, HALF_ROWS), :] = rows[:, first : first + HALF_D]
        lane = WIDTH + first // 2
        acc = to_f32(rows[:, lane : lane + 1]) + to_f32(rows[:, lane + 32 : lane + 33])
        for k in range(HALF_ROWS // HALF_D):
            part = line(acc[k * HALF_D : (k + 1) * HALF_D])
            row_acc_out[:, pl.ds(pl.multiple_of(start + k * HALF_D, HALF_D), HALF_D)] = part
    col_out[0] = cols[:, :HALF_D]
    acc = to_f32(cols[:, HALF_D : HALF_D + 1]) + to_f32(cols[:, HALF_D + 64 : HALF_D + 65])
    for k in range(SIDE // HALF_D):
        part = slice(k * HALF_D, (k + 1) * HALF_D)
        col_acc_out[:, part] = line(acc[part])


def on_device(kernel, at, operands, shapes, micros, vmem_mib=4, scratch=()):
    vmem = pl.BlockSpec(memory_space=pltpu.VMEM)
    return pl.pallas_call(
        kernel,
        in_specs=[pl.BlockSpec(memory_space=pltpu.SMEM)] + [vmem] * len(operands),
        out_specs=[vmem] * len(shapes),
        out_shape=shapes,
        scratch_shapes=scratch,
        cost_estimate=pl.CostEstimate(flops=micros * 10**9, bytes_accessed=1 << 18, transcendentals=0),
        compiler_params=pltpu.CompilerParams(vmem_limit_bytes=vmem_mib << 20),
    )(at, *operands)


def bf16(*shape):
    return jax.ShapeDtypeStruct(shape, jnp.bfloat16)


def f32(*shape):
    return jax.ShapeDtypeStruct(shape, jnp.float32)


def shards(row_emb, col_emb, row_acc, col_acc, counts, live_rows, row_marg, col_marg):
    d, r, c = (lax.axis_index(a) for a in ("dim", "row", "col"))
    core, quad, y = r % 2, (r // 2) % 4, c % 2
    row_emb, col_emb = row_emb[0], col_emb[0]
    col_part = core * 4 + quad
    live_here = live_rows[0, 0] - d * HALF_ROWS
    at = jnp.stack([d, c, core, col_part, y, live_here]).astype(jnp.int32)

    def rows_at(block, start, size):
        return lax.dynamic_slice_in_dim(block, start, size, 0)

    sent = jnp.concatenate(
        [
            rows_at(col_emb, col_part * COL_PART, COL_PART),
            rows_at(row_emb, (1 - d) * HALF_ROWS + y * ROW_PAIR, ROW_PAIR),
        ]
    )
    got = lax.ppermute(sent, "dim", DIM_SWAP)

    log_total = jnp.log(jnp.sum(row_marg).astype(jnp.float32))
    own_marg = lax.dynamic_index_in_dim(row_marg, r, 0, False)
    row_logs = jnp.log(rows_at(own_marg, d * HALF_ROWS, HALF_ROWS).astype(jnp.float32))
    col_logs = jnp.log(lax.dynamic_index_in_dim(col_marg, c, 0, False).astype(jnp.float32))
    shift_log = log_total - row_logs[:, None] - col_logs[None, :]
    tile = counts[0, 0]
    count_f = tile.astype(jnp.float32)
    weight = jnp.where(tile > 0, (0.1 + 0.25 * jnp.sqrt(count_f)) / SIDE, 0.0)
    target = jnp.log(jnp.maximum(count_f, 1.0)) + shift_log
    row_acc = rows_at(row_acc[0], d * HALF_ROWS + c * ROW_PART, ROW_PART)[None]
    col_acc = rows_at(col_acc[0], col_part * COL_PART, COL_PART)[None]

    there = lax.ppermute(got[COL_PART:], "col", Y_SWAP)
    (shared,) = on_device(share_kernel, at, (got,), (bf16(4, COL_PART, HALF_D),), 1)
    col_other = lax.all_to_all(shared, "row", 0, 0, axis_index_groups=Z_QUADS)
    (there,) = on_device(
        same_kernel, at, (there,), (bf16(ROW_PAIR, HALF_D),), C_SHARE
    )
    there, col_other = lax.optimization_barrier((there, col_other))
    col_other = lax.all_gather(col_other, "row", tiled=True, axis_index_groups=CORE_PAIRS)
    col_other = col_other.reshape(SIDE, HALF_D)
    weight, target, row_acc, col_acc = lax.optimization_barrier((weight, target, row_acc, col_acc))

    terms = (bf16(HALF_ROWS, WIDTH), bf16(HALF_ROWS, WIDTH), bf16(HALF_ROWS, WIDTH))
    for step in range(STEPS):
        last = step == STEPS - 1
        if step == 0:
            kept, given, row_term, rows, cols = on_device(
                first_tile_kernel,
                at,
                (row_emb, got, there, col_emb, col_other, weight, target),
                terms + (bf16(HALF_ROWS, WIDTH), bf16(SIDE, WIDTH)),
                3,
                24,
                [pltpu.VMEM((SIDE, WIDTH), jnp.float32)],
            )
        else:
            kept, given, row_term = on_device(
                tile_terms,
                at,
                (rows, cols, weight, target),
                terms,
                3,
                24,
                [pltpu.VMEM((SIDE, WIDTH), jnp.float32)],
            )

        pair = lax.all_gather(given, "row", axis_index_groups=CORE_PAIRS)
        (half,) = on_device(half_kernel, at, (kept, pair), (bf16(4, COL_PART, WIDTH),), 1)
        parts = lax.all_to_all(half, "row", 0, 0, axis_index_groups=Z_QUADS)
        (near,) = on_device(near_kernel, at, (parts,), (bf16(COL_PART, WIDTH),), 1)
        row_term, near = lax.optimization_barrier((row_term, near))
        far = lax.ppermute(near, "row", FAR_Z)

        row_parts = lax.all_to_all(row_term.reshape(N_COL, ROW_PART, WIDTH), "col", 0, 0)
        (near,) = on_device(pair_kernel, at, (near, far), (bf16(COL_PART, WIDTH),), C_PAIR)
        far = lax.ppermute(near, "dim", DIM_SWAP)
        if not last:
            rows, row_acc = on_device(
                row_kernel,
                at,
                (row_parts, row_acc, rows),
                (bf16(N_COL, ROW_PART, WIDTH), f32(ROW_PART, 1)),
                C_ROW,
            )
            rows = lax.all_to_all(rows, "col", 0, 0).reshape(HALF_ROWS, WIDTH)
            cols, col_acc = on_device(
                col_kernel,
                at,
                (near, far, col_acc, cols),
                (bf16(4, COL_PART, WIDTH), f32(COL_PART, 1)),
                C_COL,
            )
            rows, cols = lax.optimization_barrier((rows, cols))
            cols = lax.all_to_all(cols, "row", 0, 0, axis_index_groups=Z_QUADS)
            cols = lax.all_gather(cols, "row", tiled=True, axis_index_groups=CORE_PAIRS)
            cols = cols.reshape(SIDE, WIDTH)
            continue

        kept, sent = on_device(
            row_last_kernel,
            at,
            (row_parts, row_acc, rows),
            (bf16(ROW_PART, WIDTH), bf16(ROW_PART, WIDTH)),
            C_ROW_LAST,
        )
        rows_far = lax.ppermute(sent, "dim", DIM_SWAP)
        (cols,) = on_device(
            col_last_kernel, at, (near, far, col_acc, cols), (bf16(4, COL_PART, WIDTH),), C_COL_LAST
        )
        cols = lax.all_to_all(cols, "row", 0, 0, axis_index_groups=Z_QUADS)
        (rows,) = on_device(
            pack_kernel, at, (kept, rows_far), (bf16(N_COL, ROW_PART, WIDTH + HALF_D),), C_PACK
        )
        rows, cols = lax.optimization_barrier((rows, cols))
        rows = lax.all_to_all(rows, "col", 0, 0)
        cols = lax.all_gather(cols, "row", tiled=True, axis_index_groups=CORE_PAIRS)
        rows, cols = lax.optimization_barrier((rows, cols))

    rows = rows.reshape(HALF_ROWS, WIDTH + HALF_D)
    cols = cols.reshape(SIDE, WIDTH)
    return on_device(
        out_kernel,
        at,
        (rows, cols),
        (bf16(1, SIDE, HALF_D), f32(1, SIDE), bf16(1, SIDE, HALF_D), f32(1, SIDE)),
        1,
    )


def solution(mesh):
    return jax.shard_map(
        shards,
        mesh=mesh,
        in_specs=(
            P("row", None, "dim"),
            P("col", None, "dim"),
            P("row", None),
            P("col", None),
            P("row", "col", "dim", None),
            P("row", "col"),
            P(),
            P(),
        ),
        out_specs=(P("row", None, "dim"), P("row", None), P("col", None, "dim"), P("col", None)),
        check_vma=False,
    )
```

```python
import jax
import jax.numpy as jnp
from jax import lax
from jax.experimental import pallas as pl
from jax.experimental.pallas import tpu as pltpu
from jax.sharding import PartitionSpec as P

STEPS = 2
LEARN_RATE = 0.1
SIDE = 1024
HALF_ROWS = 512
WIDTH = 256
HALF_D = 128
N_COL = 16
ROW_PART = HALF_ROWS // N_COL
COL_PART = 128
ROW_PAIR = 256
TILE_ROWS = 256

C_COUNTS, C_SHARE, C_PAIR, C_ROW, C_COL, C_ROW_LAST, C_COL_LAST, C_PACK, C_QUAD, C_OUT = 5, 20, 20, 1, 20, 1, 20, 20, 20, 1

CORE_PAIRS = [[2 * z, 2 * z + 1] for z in range(8)]
Z_QUADS = [[2 * (4 * h + k) + core for k in range(4)] for h in range(2) for core in range(2)]
FAR_Z = [(i, i ^ 8) for i in range(16)]
IN_QUAD = [[(i, i ^ (2 * k)) for i in range(16)] for k in range(1, 4)]
Y_SWAP = [(i, i ^ 1) for i in range(16)]
DIM_SWAP = [(0, 1), (1, 0)]

AT_DIM, AT_ROW, AT_COL, AT_CORE, AT_COL_PART, AT_Y, AT_LIVE = range(7)


def to_f32(block):
    return block.astype(jnp.float32)


def swap_halves(block):
    return jnp.concatenate([block[:, HALF_D:], block[:, :HALF_D]], axis=1)


def diagonal(n):
    return lax.broadcasted_iota(jnp.int32, (n, n), 0) == lax.broadcasted_iota(jnp.int32, (n, n), 1)


def column(values, start, n):
    shape = (n, values.shape[1])
    wanted = lax.broadcasted_iota(jnp.int32, shape, 1) == lax.broadcasted_iota(jnp.int32, shape, 0) + start
    return jnp.sum(jnp.where(wanted, values, 0.0), axis=1, keepdims=True)


def line(acc):
    return jnp.sum(jnp.where(diagonal(acc.shape[0]), acc, 0.0), axis=0, keepdims=True)


def adagrad(total, acc, emb):
    squares = total * total
    square = jnp.sum(squares[:, :HALF_D] + squares[:, HALF_D:], axis=1, keepdims=True)
    acc = acc + square / WIDTH
    emb = to_f32(emb) - LEARN_RATE * total / jnp.sqrt(acc)
    return emb.astype(jnp.bfloat16), acc


def acc_lanes(acc, start, width):
    high = to_f32(acc.astype(jnp.bfloat16))
    lane = lax.broadcasted_iota(jnp.int32, (acc.shape[0], HALF_D), 1) - start
    part = jnp.where(lane < width, high, acc - high)
    return jnp.where((lane >= 0) & (lane < 2 * width), part, 0.0).astype(jnp.bfloat16)


def block_at(ref, index, size):
    return ref[pl.ds(pl.multiple_of(index * size, size), size), :]


def counts_kernel(at, counts, row_marg, col_marg, weight, target):
    marg = row_marg[...]
    high, low = to_f32(marg >> 10), to_f32(marg & 1023)
    high, low = (jnp.sum(jnp.sum(m, axis=0, keepdims=True), axis=1, keepdims=True) for m in (high, low))
    log_total = jnp.log(high * 1024.0 + low)
    col_logs = jnp.log(to_f32(col_marg[pl.ds(at[AT_COL], 1), :]))
    start = pl.multiple_of(at[AT_DIM] * HALF_ROWS, HALF_ROWS)
    row_logs = jnp.log(to_f32(row_marg[pl.ds(at[AT_ROW], 1), pl.ds(start, HALF_ROWS)]))
    for part in range(HALF_ROWS // HALF_D):
        here = slice(part * HALF_D, (part + 1) * HALF_D)
        shift = log_total - column(row_logs[:, here], 0, HALF_D) - col_logs
        tile = counts[here, :]
        count = to_f32(tile)
        weight[here, :] = jnp.where(tile > 0, (0.1 + 0.25 * jnp.sqrt(count)) / SIDE, 0.0)
        target[here, :] = jnp.log(jnp.maximum(count, 1.0)) + shift


def share_kernel(at, got, out):
    out[...] = jnp.broadcast_to(got[:COL_PART, :][None], out.shape)


def tile_terms(at, rows, cols, weight, target, kept, given, row_term, row_was, col_was, col_sum):
    row_was[...] = block_at(rows, at[AT_COL], ROW_PART)
    col_was[...] = block_at(cols, at[AT_COL_PART], COL_PART)
    cols_all = cols[...]
    for part in range(HALF_ROWS // TILE_ROWS):
        here = slice(part * TILE_ROWS, (part + 1) * TILE_ROWS)
        rows_here = rows[here, :]
        scores = lax.dot_general(
            rows_here, cols_all, (((1,), (1,)), ((), ())), preferred_element_type=jnp.float32
        )
        gap = scores - target[here, :]
        scale = weight[here, :]
        sigmoid = (0.5 / SIDE) * jnp.tanh(0.5 * gap) + 0.5 / SIDE
        cell = jnp.where(scale > 0, scale * gap, sigmoid)
        grad = cell.astype(jnp.bfloat16)
        live = lax.broadcasted_iota(jnp.int32, (TILE_ROWS, WIDTH), 0) + part * TILE_ROWS < at[AT_LIVE]
        row_sum = jnp.dot(grad, cols_all, preferred_element_type=jnp.float32)
        row_term[here, :] = jnp.where(live, row_sum, 0.0).astype(jnp.bfloat16)
        live_rows = jnp.where(live, to_f32(rows_here), 0.0).astype(jnp.bfloat16)
        term = lax.dot_general(
            grad, live_rows, (((0,), (0,)), ((), ())), preferred_element_type=jnp.float32
        )
        if part == 0:
            col_sum[...] = term
        else:
            col_sum[...] += term
    core = at[AT_CORE]
    kept[...] = block_at(col_sum, core, HALF_ROWS).astype(jnp.bfloat16)
    given[...] = block_at(col_sum, 1 - core, HALF_ROWS).astype(jnp.bfloat16)


def first_tile_kernel(
    at,
    row_emb,
    got,
    there,
    col_emb,
    col_other,
    weight,
    target,
    kept,
    given,
    row_term,
    row_was,
    col_was,
    col_sum,
    rows,
    cols,
):
    side, y = at[AT_DIM], at[AT_Y]
    rows[:, :HALF_D] = block_at(row_emb, side, HALF_ROWS)
    rows[pl.ds(pl.multiple_of(y * ROW_PAIR, ROW_PAIR), ROW_PAIR), HALF_D:] = got[COL_PART:, :]
    rows[pl.ds(pl.multiple_of((1 - y) * ROW_PAIR, ROW_PAIR), ROW_PAIR), HALF_D:] = there[...]
    cols[:, :HALF_D] = col_emb[...]
    cols[:, HALF_D:] = col_other[...]
    tile_terms(at, rows, cols, weight, target, kept, given, row_term, row_was, col_was, col_sum)


def same_kernel(at, block, out):
    out[...] = block[...]


def half_kernel(at, kept, pair, half):
    theirs = pair[pl.ds(1 - at[AT_CORE], 1), :, :][0]
    half[...] = (to_f32(kept[...]) + to_f32(theirs)).astype(jnp.bfloat16).reshape(half.shape)


def near_kernel(at, parts, near):
    near[...] = jnp.sum(to_f32(parts[...]), axis=0).astype(jnp.bfloat16)


def pair_kernel(at, mine, theirs, both):
    both[...] = (to_f32(mine[...]) + to_f32(theirs[...])).astype(jnp.bfloat16)


def row_kernel(at, parts, acc, rows, emb_out, acc_out):
    total = jnp.sum(to_f32(parts[...]), axis=0)
    emb_new, acc_out[...] = adagrad(
        total,
        column(acc[...], at[AT_DIM] * HALF_ROWS + at[AT_COL] * ROW_PART, ROW_PART),
        rows[...],
    )
    emb_out[...] = jnp.broadcast_to(emb_new[None], emb_out.shape)


def row_last_kernel(at, parts, acc, rows, kept, sent):
    total = jnp.sum(to_f32(parts[...]), axis=0)
    emb_new, acc_new = adagrad(total, acc[...], rows[...])
    kept[:, :HALF_D] = emb_new[:, :HALF_D]
    kept[:, HALF_D:] = acc_lanes(acc_new, 0, 32)
    sent[:, :HALF_D] = emb_new[:, HALF_D:]
    sent[:, HALF_D:] = acc_lanes(acc_new, 64, 32)


def col_kernel(at, mine, theirs, acc, cols, emb_out, acc_out):
    total = to_f32(mine[...]) + swap_halves(to_f32(theirs[...]))
    emb_new, acc_out[...] = adagrad(
        total,
        column(acc[...], at[AT_COL_PART] * COL_PART, COL_PART),
        cols[...],
    )
    emb_out[...] = emb_new


def col_last_kernel(at, mine, theirs, acc, cols, col_out):
    total = to_f32(mine[...]) + swap_halves(to_f32(theirs[...]))
    emb_new, acc_new = adagrad(total, acc[...], cols[...])
    col_new = jnp.concatenate([emb_new[:, :HALF_D], acc_lanes(acc_new, 0, 64)], axis=1)
    col_out[...] = col_new


def quad_kernel(at, own, one, two, three, out):
    quad = at[AT_COL_PART] % 4
    places = quad, quad + 1 - 2 * (quad % 2), (quad + 2) % 4, 3 - quad
    for place, block in zip(places, (own, one, two, three), strict=True):
        out[pl.ds(place, 1), :, :] = block[...][None]


def pack_kernel(at, kept, theirs, row_out):
    here, there = kept[...], theirs[...]
    both = (to_f32(here[:, HALF_D:]) + to_f32(there[:, HALF_D:])).astype(jnp.bfloat16)
    row_new = jnp.concatenate([here[:, :HALF_D], there[:, :HALF_D], both], axis=1)
    row_out[...] = jnp.broadcast_to(row_new[None], row_out.shape)


def row_out_kernel(at, rows, row_out, acc_out):
    side = at[AT_DIM]
    for half, first in ((side, 0), (1 - side, HALF_D)):
        start = pl.multiple_of(half * HALF_ROWS, HALF_ROWS)
        row_out[0, pl.ds(start, HALF_ROWS), :] = rows[:, first : first + HALF_D]
        lane = WIDTH + first // 2
        acc = to_f32(rows[:, lane : lane + 1]) + to_f32(rows[:, lane + 32 : lane + 33])
        for k in range(HALF_ROWS // HALF_D):
            part = line(acc[k * HALF_D : (k + 1) * HALF_D])
            acc_out[:, pl.ds(pl.multiple_of(start + k * HALF_D, HALF_D), HALF_D)] = part


def col_out_kernel(at, cols, col_out, acc_out):
    col_out[0] = cols[:, :HALF_D]
    acc = to_f32(cols[:, HALF_D : HALF_D + 1]) + to_f32(cols[:, HALF_D + 64 : HALF_D + 65])
    for k in range(SIDE // HALF_D):
        part = slice(k * HALF_D, (k + 1) * HALF_D)
        acc_out[:, part] = line(acc[part])


def on_device(kernel, at, operands, shapes, micros, vmem_mib=2, scratch=()):
    vmem = pl.BlockSpec(memory_space=pltpu.VMEM)
    return pl.pallas_call(
        kernel,
        in_specs=[pl.BlockSpec(memory_space=pltpu.SMEM)] + [vmem] * len(operands),
        out_specs=[vmem] * len(shapes),
        out_shape=shapes,
        scratch_shapes=scratch,
        cost_estimate=pl.CostEstimate(flops=micros * 10**9, bytes_accessed=1 << 18, transcendentals=0),
        compiler_params=pltpu.CompilerParams(vmem_limit_bytes=vmem_mib << 20),
    )(at, *operands)


def bf16(*shape):
    return jax.ShapeDtypeStruct(shape, jnp.bfloat16)


def f32(*shape):
    return jax.ShapeDtypeStruct(shape, jnp.float32)


def shards(row_emb, col_emb, row_acc, col_acc, counts, live_rows, row_marg, col_marg):
    d, r, c = (lax.axis_index(a) for a in ("dim", "row", "col"))
    core, quad, y = r % 2, (r // 2) % 4, c % 2
    row_emb, col_emb = row_emb[0], col_emb[0]
    col_part = core * 4 + quad
    live_here = live_rows[0, 0] - d * HALF_ROWS
    at = jnp.stack([d, r, c, core, col_part, y, live_here]).astype(jnp.int32)

    def rows_at(block, start, size):
        return lax.dynamic_slice_in_dim(block, start, size, 0)

    sent = jnp.concatenate(
        [
            rows_at(col_emb, col_part * COL_PART, COL_PART),
            rows_at(row_emb, (1 - d) * HALF_ROWS + y * ROW_PAIR, ROW_PAIR),
        ]
    )
    got = lax.ppermute(sent, "dim", DIM_SWAP)

    weight, target = on_device(
        counts_kernel,
        at,
        (counts[0, 0], row_marg, col_marg),
        (f32(HALF_ROWS, SIDE), f32(HALF_ROWS, SIDE)),
        C_COUNTS,
        16,
    )
    there = lax.ppermute(got[COL_PART:], "col", Y_SWAP)
    (shared,) = on_device(share_kernel, at, (got,), (bf16(4, COL_PART, HALF_D),), 1)
    col_other = lax.all_to_all(shared, "row", 0, 0, axis_index_groups=Z_QUADS)
    (there,) = on_device(
        same_kernel, at, (there,), (bf16(ROW_PAIR, HALF_D),), C_SHARE
    )
    there, col_other = lax.optimization_barrier((there, col_other))
    col_other = lax.all_gather(col_other, "row", tiled=True, axis_index_groups=CORE_PAIRS)
    col_other = col_other.reshape(SIDE, HALF_D)

    terms = (bf16(HALF_ROWS, WIDTH),) * 3 + (bf16(ROW_PART, WIDTH), bf16(COL_PART, WIDTH))
    col_sum = pltpu.VMEM((SIDE, WIDTH), jnp.float32)
    for step in range(STEPS):
        last = step == STEPS - 1
        if step == 0:
            kept, given, row_term, row_was, col_was = on_device(
                first_tile_kernel,
                at,
                (row_emb, got, there, col_emb, col_other, weight, target),
                terms,
                3,
                16,
                [col_sum, pltpu.VMEM((HALF_ROWS, WIDTH), jnp.bfloat16), pltpu.VMEM((SIDE, WIDTH), jnp.bfloat16)],
            )
        else:
            kept, given, row_term, row_was, col_was = on_device(
                tile_terms,
                at,
                (rows, cols, weight, target),
                terms,
                3,
                16,
                [col_sum],
            )

        pair = lax.all_gather(given, "row", axis_index_groups=CORE_PAIRS)
        (half,) = on_device(half_kernel, at, (kept, pair), (bf16(4, COL_PART, WIDTH),), 1)
        parts = lax.all_to_all(half, "row", 0, 0, axis_index_groups=Z_QUADS)
        (near,) = on_device(near_kernel, at, (parts,), (bf16(COL_PART, WIDTH),), 1)
        row_term, near = lax.optimization_barrier((row_term, near))
        far = lax.ppermute(near, "row", FAR_Z)

        row_parts = lax.all_to_all(row_term.reshape(N_COL, ROW_PART, WIDTH), "col", 0, 0)
        (near,) = on_device(pair_kernel, at, (near, far), (bf16(COL_PART, WIDTH),), C_PAIR)
        far = lax.ppermute(near, "dim", DIM_SWAP)
        if not last:
            rows, row_acc = on_device(
                row_kernel,
                at,
                (row_parts, row_acc, row_was),
                (bf16(N_COL, ROW_PART, WIDTH), f32(ROW_PART, 1)),
                C_ROW,
            )
            rows = lax.all_to_all(rows, "col", 0, 0).reshape(HALF_ROWS, WIDTH)
            cols, col_acc = on_device(
                col_kernel,
                at,
                (near, far, col_acc, col_was),
                (bf16(COL_PART, WIDTH), f32(COL_PART, 1)),
                C_COL,
            )
            blocks = [cols] + [lax.ppermute(cols, "row", swap) for swap in IN_QUAD]
            rows, *blocks = lax.optimization_barrier((rows, *blocks))
            (cols,) = on_device(quad_kernel, at, blocks, (bf16(4, COL_PART, WIDTH),), C_QUAD)
            cols = lax.all_gather(cols, "row", tiled=True, axis_index_groups=CORE_PAIRS)
            cols = cols.reshape(SIDE, WIDTH)
            continue

        kept, sent = on_device(
            row_last_kernel,
            at,
            (row_parts, row_acc, row_was),
            (bf16(ROW_PART, WIDTH), bf16(ROW_PART, WIDTH)),
            C_ROW_LAST,
        )
        rows_far = lax.ppermute(sent, "dim", DIM_SWAP)
        (cols,) = on_device(
            col_last_kernel, at, (near, far, col_acc, col_was), (bf16(COL_PART, WIDTH),), C_COL_LAST
        )
        blocks = [cols] + [lax.ppermute(cols, "row", swap) for swap in IN_QUAD]
        (rows,) = on_device(
            pack_kernel, at, (kept, rows_far), (bf16(N_COL, ROW_PART, WIDTH + HALF_D),), C_PACK
        )
        rows = lax.all_to_all(rows, "col", 0, 0)
        (cols,) = on_device(quad_kernel, at, blocks, (bf16(4, COL_PART, WIDTH),), C_QUAD)
        cols = lax.all_gather(cols, "row", tiled=True, axis_index_groups=CORE_PAIRS)

    shapes = bf16(1, SIDE, HALF_D), f32(1, SIDE)
    cols = on_device(col_out_kernel, at, (cols.reshape(SIDE, WIDTH),), shapes, C_OUT)
    rows, *cols = lax.optimization_barrier((rows, *cols))
    rows = rows.reshape(HALF_ROWS, WIDTH + HALF_D)
    return (*on_device(row_out_kernel, at, (rows,), shapes, 1), *cols)


def solution(mesh):
    return jax.shard_map(
        shards,
        mesh=mesh,
        in_specs=(
            P("row", None, "dim"),
            P("col", None, "dim"),
            P("row", None),
            P("col", None),
            P("row", "col", "dim", None),
            P("row", "col"),
            P(),
            P(),
        ),
        out_specs=(P("row", None, "dim"), P("row", None), P("col", None, "dim"), P("col", None)),
        check_vma=False,
    )
```

```python
import jax
import jax.numpy as jnp
from jax import lax
from jax.experimental import pallas as pl
from jax.experimental.pallas import tpu as pltpu
from jax.sharding import PartitionSpec as P

STEPS = 2
LEARN_RATE = 0.1
SIDE = 1024
HALF_ROWS = 512
WIDTH = 256
HALF_D = 128
N_COL = 16
ROW_PART = HALF_ROWS // N_COL
COL_PART = 128
ROW_PAIR = 256
TILE_ROWS = 256

C_FIRST, C_SAME, C_PAIR, C_ROW, C_COL, C_ROW_LAST, C_COL_LAST, C_PACK, C_QUAD, C_OUT = 5, 20, 20, 1, 20, 1, 20, 20, 20, 1

CORE_PAIRS = [[2 * z, 2 * z + 1] for z in range(8)]
Z_QUADS = [[2 * (4 * h + k) + core for k in range(4)] for h in range(2) for core in range(2)]


def far_pairs():
    def place(z, core):
        return 2 * (2 * (z % 8) + core) + z // 8

    pairs = []
    for z in range(16):
        up, down = (z + 4) % 16, (z - 4) % 16
        first = z // 4 % 2 == 0
        pairs += [(place(z, 0), place(up if first else down, 0)), (place(z, 1), place(down if first else up, 1))]
    return sorted(pairs)


FAR_Z = far_pairs()
IN_QUAD = [[(i, i ^ (2 * k)) for i in range(16)] for k in range(1, 4)]
Y_SWAP = [(i, i ^ 1) for i in range(16)]
DIM_SWAP = [(0, 1), (1, 0)]

AT_DIM, AT_ROW, AT_COL, AT_CORE, AT_COL_PART, AT_Y, AT_LIVE = range(7)


def to_f32(block):
    return block.astype(jnp.float32)


def swap_halves(block):
    return jnp.concatenate([block[:, HALF_D:], block[:, :HALF_D]], axis=1)


def diagonal(n):
    return lax.broadcasted_iota(jnp.int32, (n, n), 0) == lax.broadcasted_iota(jnp.int32, (n, n), 1)


def column(values, start, n):
    shape = (n, values.shape[1])
    wanted = lax.broadcasted_iota(jnp.int32, shape, 1) == lax.broadcasted_iota(jnp.int32, shape, 0) + start
    return jnp.sum(jnp.where(wanted, values, 0.0), axis=1, keepdims=True)


def line(acc):
    return jnp.sum(jnp.where(diagonal(acc.shape[0]), acc, 0.0), axis=0, keepdims=True)


def adagrad(total, acc, emb):
    squares = total * total
    square = jnp.sum(squares[:, :HALF_D] + squares[:, HALF_D:], axis=1, keepdims=True)
    acc = acc + square / WIDTH
    emb = to_f32(emb) - LEARN_RATE * total / jnp.sqrt(acc)
    return emb.astype(jnp.bfloat16), acc


def acc_lanes(acc, start, width):
    high = to_f32(acc.astype(jnp.bfloat16))
    lane = lax.broadcasted_iota(jnp.int32, (acc.shape[0], HALF_D), 1) - start
    part = jnp.where(lane < width, high, acc - high)
    return jnp.where((lane >= 0) & (lane < 2 * width), part, 0.0).astype(jnp.bfloat16)


def block_at(ref, index, size):
    return ref[pl.ds(pl.multiple_of(index * size, size), size), :]


def count_terms(at, counts, row_marg, col_marg, weight, target):
    marg = row_marg[...]
    high, low = to_f32(marg >> 10), to_f32(marg & 1023)
    high, low = (jnp.sum(jnp.sum(m, axis=0, keepdims=True), axis=1, keepdims=True) for m in (high, low))
    log_total = jnp.log(high * 1024.0 + low)
    col_logs = jnp.log(to_f32(col_marg[pl.ds(at[AT_COL], 1), :]))
    start = pl.multiple_of(at[AT_DIM] * HALF_ROWS, HALF_ROWS)
    row_logs = jnp.log(to_f32(row_marg[pl.ds(at[AT_ROW], 1), pl.ds(start, HALF_ROWS)]))
    for part in range(HALF_ROWS // HALF_D):
        here = slice(part * HALF_D, (part + 1) * HALF_D)
        shift = log_total - column(row_logs[:, here], 0, HALF_D) - col_logs
        tile = counts[here, :]
        count = to_f32(tile)
        weight[here, :] = jnp.where(tile > 0, (0.1 + 0.25 * jnp.sqrt(count)) / SIDE, 0.0)
        target[here, :] = jnp.log(jnp.maximum(count, 1.0)) + shift


def share_kernel(at, got, out):
    out[...] = jnp.broadcast_to(got[...][None], out.shape)


def tile_terms(at, rows, cols, weight, target, kept, given, row_term, row_was, col_was, col_sum):
    row_was[...] = block_at(rows, at[AT_COL], ROW_PART)
    col_was[...] = block_at(cols, at[AT_COL_PART], COL_PART)
    cols_all = cols[...]
    for part in range(HALF_ROWS // TILE_ROWS):
        here = slice(part * TILE_ROWS, (part + 1) * TILE_ROWS)
        rows_here = rows[here, :]
        scores = lax.dot_general(
            rows_here, cols_all, (((1,), (1,)), ((), ())), preferred_element_type=jnp.float32
        )
        gap = scores - target[here, :]
        scale = weight[here, :]
        sigmoid = (0.5 / SIDE) * jnp.tanh(0.5 * gap) + 0.5 / SIDE
        cell = jnp.where(scale > 0, scale * gap, sigmoid)
        grad = cell.astype(jnp.bfloat16)
        live = lax.broadcasted_iota(jnp.int32, (TILE_ROWS, WIDTH), 0) + part * TILE_ROWS < at[AT_LIVE]
        row_sum = jnp.dot(grad, cols_all, preferred_element_type=jnp.float32)
        row_term[here, :] = jnp.where(live, row_sum, 0.0).astype(jnp.bfloat16)
        live_rows = jnp.where(live, to_f32(rows_here), 0.0).astype(jnp.bfloat16)
        term = lax.dot_general(
            grad, live_rows, (((0,), (0,)), ((), ())), preferred_element_type=jnp.float32
        )
        if part == 0:
            col_sum[...] = term
        else:
            col_sum[...] += term
    core = at[AT_CORE]
    kept[...] = block_at(col_sum, core, HALF_ROWS).astype(jnp.bfloat16)
    given[...] = block_at(col_sum, 1 - core, HALF_ROWS).astype(jnp.bfloat16)


def first_tile_kernel(
    at,
    row_emb,
    got,
    there,
    col_emb,
    col_other,
    counts,
    row_marg,
    col_marg,
    kept,
    given,
    row_term,
    row_was,
    col_was,
    weight,
    target,
    col_sum,
    rows,
    cols,
):
    side, y = at[AT_DIM], at[AT_Y]
    rows[:, :HALF_D] = block_at(row_emb, side, HALF_ROWS)
    rows[pl.ds(pl.multiple_of(y * ROW_PAIR, ROW_PAIR), ROW_PAIR), HALF_D:] = got[...]
    rows[pl.ds(pl.multiple_of((1 - y) * ROW_PAIR, ROW_PAIR), ROW_PAIR), HALF_D:] = there[...]
    cols[:, :HALF_D] = col_emb[...]
    cols[:, HALF_D:] = col_other[...]
    count_terms(at, counts, row_marg, col_marg, weight, target)
    tile_terms(at, rows, cols, weight, target, kept, given, row_term, row_was, col_was, col_sum)


def same_kernel(at, block, out):
    out[...] = block[...]


def half_kernel(at, kept, pair, half):
    theirs = pair[pl.ds(1 - at[AT_CORE], 1), :, :][0]
    half[...] = (to_f32(kept[...]) + to_f32(theirs)).astype(jnp.bfloat16).reshape(half.shape)


def near_kernel(at, parts, near):
    near[...] = jnp.sum(to_f32(parts[...]), axis=0).astype(jnp.bfloat16)


def pair_kernel(at, mine, theirs, both):
    block = to_f32(theirs[...])
    block = jnp.where(at[AT_CORE] == 1, swap_halves(block), block)
    both[...] = (to_f32(mine[...]) + block).astype(jnp.bfloat16)


def row_kernel(at, parts, acc, rows, emb_out, acc_out):
    total = jnp.sum(to_f32(parts[...]), axis=0)
    emb_new, acc_out[...] = adagrad(
        total,
        column(acc[...], at[AT_DIM] * HALF_ROWS + at[AT_COL] * ROW_PART, ROW_PART),
        rows[...],
    )
    emb_out[...] = jnp.broadcast_to(emb_new[None], emb_out.shape)


def row_last_kernel(at, parts, acc, rows, kept, sent):
    total = jnp.sum(to_f32(parts[...]), axis=0)
    emb_new, acc_new = adagrad(total, acc[...], rows[...])
    kept[:, :HALF_D] = emb_new[:, :HALF_D]
    kept[:, HALF_D:] = acc_lanes(acc_new, 0, 32)
    sent[:, :HALF_D] = emb_new[:, HALF_D:]
    sent[:, HALF_D:] = acc_lanes(acc_new, 64, 32)


def col_kernel(at, mine, theirs, acc, cols, emb_out, acc_out):
    total = to_f32(mine[...]) + swap_halves(to_f32(theirs[...]))
    emb_new, acc_out[...] = adagrad(
        total,
        column(acc[...], at[AT_COL_PART] * COL_PART, COL_PART),
        cols[...],
    )
    emb_out[...] = emb_new


def col_last_kernel(at, mine, theirs, acc, cols, col_out):
    total = to_f32(mine[...]) + swap_halves(to_f32(theirs[...]))
    emb_new, acc_new = adagrad(total, acc[...], cols[...])
    col_new = jnp.concatenate([emb_new[:, :HALF_D], acc_lanes(acc_new, 0, 64)], axis=1)
    col_out[...] = col_new


def quad_kernel(at, own, one, two, three, out):
    quad = at[AT_COL_PART] % 4
    places = quad, quad + 1 - 2 * (quad % 2), (quad + 2) % 4, 3 - quad
    for place, block in zip(places, (own, one, two, three), strict=True):
        out[pl.ds(place, 1), :, :] = block[...][None]


def pack_kernel(at, kept, theirs, row_out):
    here, there = kept[...], theirs[...]
    both = (to_f32(here[:, HALF_D:]) + to_f32(there[:, HALF_D:])).astype(jnp.bfloat16)
    row_new = jnp.concatenate([here[:, :HALF_D], there[:, :HALF_D], both], axis=1)
    row_out[...] = jnp.broadcast_to(row_new[None], row_out.shape)


def row_out_kernel(at, rows, row_out, acc_out):
    side = at[AT_DIM]
    for half, first in ((side, 0), (1 - side, HALF_D)):
        start = pl.multiple_of(half * HALF_ROWS, HALF_ROWS)
        row_out[0, pl.ds(start, HALF_ROWS), :] = rows[:, first : first + HALF_D]
        lane = WIDTH + first // 2
        acc = to_f32(rows[:, lane : lane + 1]) + to_f32(rows[:, lane + 32 : lane + 33])
        for k in range(HALF_ROWS // HALF_D):
            part = line(acc[k * HALF_D : (k + 1) * HALF_D])
            acc_out[:, pl.ds(pl.multiple_of(start + k * HALF_D, HALF_D), HALF_D)] = part


def col_out_kernel(at, cols, col_out, acc_out):
    col_out[0] = cols[:, :HALF_D]
    acc = to_f32(cols[:, HALF_D : HALF_D + 1]) + to_f32(cols[:, HALF_D + 64 : HALF_D + 65])
    for k in range(SIDE // HALF_D):
        part = slice(k * HALF_D, (k + 1) * HALF_D)
        acc_out[:, part] = line(acc[part])


def on_device(kernel, at, operands, shapes, micros, vmem_mib=2, scratch=()):
    vmem = pl.BlockSpec(memory_space=pltpu.VMEM)
    return pl.pallas_call(
        kernel,
        in_specs=[pl.BlockSpec(memory_space=pltpu.SMEM)] + [vmem] * len(operands),
        out_specs=[vmem] * len(shapes),
        out_shape=shapes,
        scratch_shapes=scratch,
        cost_estimate=pl.CostEstimate(flops=micros * 10**9, bytes_accessed=1 << 18, transcendentals=0),
        compiler_params=pltpu.CompilerParams(vmem_limit_bytes=vmem_mib << 20),
    )(at, *operands)


def bf16(*shape):
    return jax.ShapeDtypeStruct(shape, jnp.bfloat16)


def f32(*shape):
    return jax.ShapeDtypeStruct(shape, jnp.float32)


def shards(row_emb, col_emb, row_acc, col_acc, counts, live_rows, row_marg, col_marg):
    d, r, c = (lax.axis_index(a) for a in ("dim", "row", "col"))
    core, quad, y = r % 2, (r // 2) % 4, c % 2
    row_emb, col_emb = row_emb[0], col_emb[0]
    col_part = core * 4 + quad
    live_here = live_rows[0, 0] - d * HALF_ROWS
    at = jnp.stack([d, r, c, core, col_part, y, live_here]).astype(jnp.int32)

    def rows_at(block, start, size):
        return lax.dynamic_slice_in_dim(block, start, size, 0)

    col_got = lax.ppermute(rows_at(col_emb, col_part * COL_PART, COL_PART), "dim", DIM_SWAP)
    row_got = lax.ppermute(
        rows_at(row_emb, (1 - d) * HALF_ROWS + y * ROW_PAIR, ROW_PAIR), "dim", DIM_SWAP
    )
    (shared,) = on_device(share_kernel, at, (col_got,), (bf16(4, COL_PART, HALF_D),), 1)
    col_other = lax.all_to_all(shared, "row", 0, 0, axis_index_groups=Z_QUADS)
    (row_got,) = on_device(same_kernel, at, (row_got,), (bf16(ROW_PAIR, HALF_D),), C_SAME)
    there = lax.ppermute(row_got, "col", Y_SWAP)
    col_other = lax.all_gather(col_other, "row", tiled=True, axis_index_groups=CORE_PAIRS)
    col_other = col_other.reshape(SIDE, HALF_D)

    terms = (bf16(HALF_ROWS, WIDTH),) * 3 + (bf16(ROW_PART, WIDTH), bf16(COL_PART, WIDTH))
    col_sum = pltpu.VMEM((SIDE, WIDTH), jnp.float32)
    for step in range(STEPS):
        last = step == STEPS - 1
        if step == 0:
            kept, given, row_term, row_was, col_was, weight, target = on_device(
                first_tile_kernel,
                at,
                (row_emb, row_got, there, col_emb, col_other, counts[0, 0], row_marg, col_marg),
                terms + (f32(HALF_ROWS, SIDE),) * 2,
                3,
                16,
                [col_sum, pltpu.VMEM((HALF_ROWS, WIDTH), jnp.bfloat16), pltpu.VMEM((SIDE, WIDTH), jnp.bfloat16)],
            )
        else:
            kept, given, row_term, row_was, col_was = on_device(
                tile_terms,
                at,
                (rows, cols, weight, target),
                terms,
                3,
                16,
                [col_sum],
            )

        pair = lax.all_gather(given, "row", axis_index_groups=CORE_PAIRS)
        (half,) = on_device(half_kernel, at, (kept, pair), (bf16(4, COL_PART, WIDTH),), 1)
        parts = lax.all_to_all(half, "row", 0, 0, axis_index_groups=Z_QUADS)
        (near,) = on_device(near_kernel, at, (parts,), (bf16(COL_PART, WIDTH),), 1)
        row_term, near = lax.optimization_barrier((row_term, near))
        far = lax.ppermute(near, ("row", "dim"), FAR_Z)

        row_parts = lax.all_to_all(row_term.reshape(N_COL, ROW_PART, WIDTH), "col", 0, 0)
        (near,) = on_device(pair_kernel, at, (near, far), (bf16(COL_PART, WIDTH),), C_PAIR)
        far = lax.ppermute(near, "dim", DIM_SWAP)
        if not last:
            rows, row_acc = on_device(
                row_kernel,
                at,
                (row_parts, row_acc, row_was),
                (bf16(N_COL, ROW_PART, WIDTH), f32(ROW_PART, 1)),
                C_ROW,
            )
            rows = lax.all_to_all(rows, "col", 0, 0).reshape(HALF_ROWS, WIDTH)
            cols, col_acc = on_device(
                col_kernel,
                at,
                (near, far, col_acc, col_was),
                (bf16(COL_PART, WIDTH), f32(COL_PART, 1)),
                C_COL,
            )
            blocks = [cols] + [lax.ppermute(cols, "row", swap) for swap in IN_QUAD]
            rows, *blocks = lax.optimization_barrier((rows, *blocks))
            (cols,) = on_device(quad_kernel, at, blocks, (bf16(4, COL_PART, WIDTH),), C_QUAD)
            cols = lax.all_gather(cols, "row", tiled=True, axis_index_groups=CORE_PAIRS)
            cols = cols.reshape(SIDE, WIDTH)
            continue

        kept, sent = on_device(
            row_last_kernel,
            at,
            (row_parts, row_acc, row_was),
            (bf16(ROW_PART, WIDTH), bf16(ROW_PART, WIDTH)),
            C_ROW_LAST,
        )
        rows_far = lax.ppermute(sent, "dim", DIM_SWAP)
        (cols,) = on_device(
            col_last_kernel, at, (near, far, col_acc, col_was), (bf16(COL_PART, WIDTH),), C_COL_LAST
        )
        blocks = [cols] + [lax.ppermute(cols, "row", swap) for swap in IN_QUAD]
        (rows,) = on_device(
            pack_kernel, at, (kept, rows_far), (bf16(N_COL, ROW_PART, WIDTH + HALF_D),), C_PACK
        )
        rows = lax.all_to_all(rows, "col", 0, 0)
        (cols,) = on_device(quad_kernel, at, blocks, (bf16(4, COL_PART, WIDTH),), C_QUAD)
        cols = lax.all_gather(cols, "row", tiled=True, axis_index_groups=CORE_PAIRS)

    shapes = bf16(1, SIDE, HALF_D), f32(1, SIDE)
    cols = on_device(col_out_kernel, at, (cols.reshape(SIDE, WIDTH),), shapes, C_OUT)
    rows, *cols = lax.optimization_barrier((rows, *cols))
    rows = rows.reshape(HALF_ROWS, WIDTH + HALF_D)
    return (*on_device(row_out_kernel, at, (rows,), shapes, 1), *cols)


def solution(mesh):
    return jax.shard_map(
        shards,
        mesh=mesh,
        in_specs=(
            P("row", None, "dim"),
            P("col", None, "dim"),
            P("row", None),
            P("col", None),
            P("row", "col", "dim", None),
            P("row", "col"),
            P(),
            P(),
        ),
        out_specs=(P("row", None, "dim"), P("row", None), P("col", None, "dim"), P("col", None)),
        check_vma=False,
    )
```

```python
import jax
import jax.numpy as jnp
from jax import lax
from jax.experimental import pallas as pl
from jax.experimental.pallas import tpu as pltpu
from jax.sharding import PartitionSpec as P

STEPS = 2
LEARN_RATE = 0.1
SIDE = 1024
HALF_ROWS = 512
WIDTH = 256
HALF_D = 128
N_COL = 16
ROW_PART = HALF_ROWS // N_COL
COL_PART = 128
ROW_PAIR = 256
TILE_ROWS = 256

C_FIRST, C_SAME, C_PAIR, C_ROW, C_COL, C_ROW_LAST, C_COL_LAST, C_PACK, C_QUAD, C_OUT = 5, 20, 20, 1, 20, 1, 20, 20, 20, 1

CORE_PAIRS = [[2 * z, 2 * z + 1] for z in range(8)]
Z_QUADS = [[2 * (4 * h + k) + core for k in range(4)] for h in range(2) for core in range(2)]


def far_pairs():
    def place(z, core):
        return 2 * (2 * (z % 8) + core) + z // 8

    pairs = []
    for z in range(16):
        up, down = (z + 4) % 16, (z - 4) % 16
        first = z // 4 % 2 == 0
        pairs += [(place(z, 0), place(up if first else down, 0)), (place(z, 1), place(down if first else up, 1))]
    return sorted(pairs)


FAR_Z = far_pairs()
IN_QUAD = [[(i, i ^ (2 * k)) for i in range(16)] for k in range(1, 4)]
Y_SWAP = [(i, i ^ 1) for i in range(16)]
DIM_SWAP = [(0, 1), (1, 0)]

AT_DIM, AT_ROW, AT_COL, AT_CORE, AT_COL_PART, AT_Y, AT_LIVE = range(7)


def to_f32(block):
    return block.astype(jnp.float32)


def swap_halves(block):
    return jnp.concatenate([block[:, HALF_D:], block[:, :HALF_D]], axis=1)


def diagonal(n):
    return lax.broadcasted_iota(jnp.int32, (n, n), 0) == lax.broadcasted_iota(jnp.int32, (n, n), 1)


def column(values, start, n):
    shape = (n, values.shape[1])
    wanted = lax.broadcasted_iota(jnp.int32, shape, 1) == lax.broadcasted_iota(jnp.int32, shape, 0) + start
    return jnp.sum(jnp.where(wanted, values, 0.0), axis=1, keepdims=True)


def line(acc):
    return jnp.sum(jnp.where(diagonal(acc.shape[0]), acc, 0.0), axis=0, keepdims=True)


def adagrad(total, acc, emb):
    squares = total * total
    square = jnp.sum(squares[:, :HALF_D] + squares[:, HALF_D:], axis=1, keepdims=True)
    acc = acc + square / WIDTH
    emb = to_f32(emb) - LEARN_RATE * total / jnp.sqrt(acc)
    return emb.astype(jnp.bfloat16), acc


def acc_lanes(acc, start, width):
    high = to_f32(acc.astype(jnp.bfloat16))
    lane = lax.broadcasted_iota(jnp.int32, (acc.shape[0], HALF_D), 1) - start
    part = jnp.where(lane < width, high, acc - high)
    return jnp.where((lane >= 0) & (lane < 2 * width), part, 0.0).astype(jnp.bfloat16)


def block_at(ref, index, size):
    return ref[pl.ds(pl.multiple_of(index * size, size), size), :]


def count_terms(at, counts, row_marg, col_marg, weight, target):
    marg = row_marg[...]
    high, low = to_f32(marg >> 10), to_f32(marg & 1023)
    high, low = (jnp.sum(jnp.sum(m, axis=0, keepdims=True), axis=1, keepdims=True) for m in (high, low))
    log_total = jnp.log(high * 1024.0 + low)
    col_logs = jnp.log(to_f32(col_marg[pl.ds(at[AT_COL], 1), :]))
    start = pl.multiple_of(at[AT_DIM] * HALF_ROWS, HALF_ROWS)
    row_logs = jnp.log(to_f32(row_marg[pl.ds(at[AT_ROW], 1), pl.ds(start, HALF_ROWS)]))
    for part in range(HALF_ROWS // HALF_D):
        here = slice(part * HALF_D, (part + 1) * HALF_D)
        shift = log_total - column(row_logs[:, here], 0, HALF_D) - col_logs
        tile = counts[here, :]
        count = to_f32(tile)
        weight[here, :] = jnp.where(tile > 0, (0.1 + 0.25 * jnp.sqrt(count)) / SIDE, 0.0)
        target[here, :] = jnp.log(jnp.maximum(count, 1.0)) + shift


def share_kernel(at, got, out):
    out[...] = jnp.broadcast_to(got[...][None], out.shape)


def tile_terms(at, rows, cols, weight, target, kept, given, row_term, row_was, col_was, col_sum):
    row_was[...] = block_at(rows, at[AT_COL], ROW_PART)
    col_was[...] = block_at(cols, at[AT_COL_PART], COL_PART)
    cols_all = cols[...]
    for part in range(HALF_ROWS // TILE_ROWS):
        here = slice(part * TILE_ROWS, (part + 1) * TILE_ROWS)
        rows_here = rows[here, :]
        scores = lax.dot_general(
            rows_here, cols_all, (((1,), (1,)), ((), ())), preferred_element_type=jnp.float32
        )
        gap = scores - target[here, :]
        scale = weight[here, :]
        sigmoid = (0.5 / SIDE) * jnp.tanh(0.5 * gap) + 0.5 / SIDE
        cell = jnp.where(scale > 0, scale * gap, sigmoid)
        grad = cell.astype(jnp.bfloat16)
        live = lax.broadcasted_iota(jnp.int32, (TILE_ROWS, WIDTH), 0) + part * TILE_ROWS < at[AT_LIVE]
        row_sum = jnp.dot(grad, cols_all, preferred_element_type=jnp.float32)
        row_term[here, :] = jnp.where(live, row_sum, 0.0).astype(jnp.bfloat16)
        live_rows = jnp.where(live, to_f32(rows_here), 0.0).astype(jnp.bfloat16)
        term = lax.dot_general(
            grad, live_rows, (((0,), (0,)), ((), ())), preferred_element_type=jnp.float32
        )
        if part == 0:
            col_sum[...] = term
        else:
            col_sum[...] += term
    core = at[AT_CORE]
    kept[...] = block_at(col_sum, core, HALF_ROWS).astype(jnp.bfloat16)
    given[...] = block_at(col_sum, 1 - core, HALF_ROWS).astype(jnp.bfloat16)


def first_tile_kernel(
    at,
    row_emb,
    got,
    there,
    col_emb,
    col_other,
    counts,
    row_marg,
    col_marg,
    kept,
    given,
    row_term,
    row_was,
    col_was,
    weight,
    target,
    col_sum,
    rows,
    cols,
):
    side, y = at[AT_DIM], at[AT_Y]
    rows[:, :HALF_D] = block_at(row_emb, side, HALF_ROWS)
    rows[pl.ds(pl.multiple_of(y * ROW_PAIR, ROW_PAIR), ROW_PAIR), HALF_D:] = got[...]
    rows[pl.ds(pl.multiple_of((1 - y) * ROW_PAIR, ROW_PAIR), ROW_PAIR), HALF_D:] = there[...]
    cols[:, :HALF_D] = col_emb[...]
    cols[:, HALF_D:] = col_other[...]
    count_terms(at, counts, row_marg, col_marg, weight, target)
    tile_terms(at, rows, cols, weight, target, kept, given, row_term, row_was, col_was, col_sum)


def same_kernel(at, block, out):
    out[...] = block[...]


def half_kernel(at, kept, pair, half):
    theirs = pair[pl.ds(1 - at[AT_CORE], 1), :, :][0]
    half[...] = (to_f32(kept[...]) + to_f32(theirs)).astype(jnp.bfloat16).reshape(half.shape)


def near_kernel(at, parts, near):
    near[...] = jnp.sum(to_f32(parts[...]), axis=0).astype(jnp.bfloat16)


def pair_kernel(at, mine, theirs, both):
    block = to_f32(theirs[...])
    block = jnp.where(at[AT_CORE] == 1, swap_halves(block), block)
    both[...] = (to_f32(mine[...]) + block).astype(jnp.bfloat16)


def row_kernel(at, parts, acc, rows, emb_out, acc_out):
    total = jnp.sum(to_f32(parts[...]), axis=0)
    emb_new, acc_out[...] = adagrad(
        total,
        column(acc[...], at[AT_DIM] * HALF_ROWS + at[AT_COL] * ROW_PART, ROW_PART),
        rows[...],
    )
    emb_out[...] = jnp.broadcast_to(emb_new[None], emb_out.shape)


def row_last_kernel(at, parts, acc, rows, kept, sent):
    total = jnp.sum(to_f32(parts[...]), axis=0)
    emb_new, acc_new = adagrad(total, acc[...], rows[...])
    kept[:, :HALF_D] = emb_new[:, :HALF_D]
    kept[:, HALF_D:] = acc_lanes(acc_new, 0, 32)
    sent[:, :HALF_D] = emb_new[:, HALF_D:]
    sent[:, HALF_D:] = acc_lanes(acc_new, 64, 32)


def col_kernel(at, mine, theirs, acc, cols, emb_out, acc_out):
    total = to_f32(mine[...]) + swap_halves(to_f32(theirs[...]))
    emb_new, acc_out[...] = adagrad(
        total,
        column(acc[...], at[AT_COL_PART] * COL_PART, COL_PART),
        cols[...],
    )
    emb_out[...] = emb_new


def col_last_kernel(at, mine, theirs, acc, cols, col_out):
    total = to_f32(mine[...]) + swap_halves(to_f32(theirs[...]))
    emb_new, acc_new = adagrad(total, acc[...], cols[...])
    col_new = jnp.concatenate([emb_new[:, :HALF_D], acc_lanes(acc_new, 0, 64)], axis=1)
    col_out[...] = col_new


def quad_kernel(at, own, one, two, three, out):
    quad = at[AT_COL_PART] % 4
    places = quad, quad + 1 - 2 * (quad % 2), (quad + 2) % 4, 3 - quad
    for place, block in zip(places, (own, one, two, three), strict=True):
        out[pl.ds(place, 1), :, :] = block[...][None]


def pack_kernel(at, kept, theirs, row_out):
    here, there = kept[...], theirs[...]
    both = (to_f32(here[:, HALF_D:]) + to_f32(there[:, HALF_D:])).astype(jnp.bfloat16)
    row_new = jnp.concatenate([here[:, :HALF_D], there[:, :HALF_D], both], axis=1)
    row_out[...] = jnp.broadcast_to(row_new[None], row_out.shape)


def row_out_kernel(at, rows, row_out, acc_out):
    side = at[AT_DIM]
    for half, first in ((side, 0), (1 - side, HALF_D)):
        start = pl.multiple_of(half * HALF_ROWS, HALF_ROWS)
        row_out[0, pl.ds(start, HALF_ROWS), :] = rows[:, first : first + HALF_D]
        lane = WIDTH + first // 2
        acc = to_f32(rows[:, lane : lane + 1]) + to_f32(rows[:, lane + 32 : lane + 33])
        for k in range(HALF_ROWS // HALF_D):
            part = line(acc[k * HALF_D : (k + 1) * HALF_D])
            acc_out[:, pl.ds(pl.multiple_of(start + k * HALF_D, HALF_D), HALF_D)] = part


def col_out_kernel(at, cols, col_out, acc_out):
    col_out[0] = cols[:, :HALF_D]
    acc = to_f32(cols[:, HALF_D : HALF_D + 1]) + to_f32(cols[:, HALF_D + 64 : HALF_D + 65])
    for k in range(SIDE // HALF_D):
        part = slice(k * HALF_D, (k + 1) * HALF_D)
        acc_out[:, part] = line(acc[part])


def on_device(kernel, at, operands, shapes, micros, vmem_mib=2, scratch=()):
    vmem = pl.BlockSpec(memory_space=pltpu.VMEM)
    return pl.pallas_call(
        kernel,
        in_specs=[pl.BlockSpec(memory_space=pltpu.SMEM)] + [vmem] * len(operands),
        out_specs=[vmem] * len(shapes),
        out_shape=shapes,
        scratch_shapes=scratch,
        cost_estimate=pl.CostEstimate(flops=micros * 10**9, bytes_accessed=1 << 18, transcendentals=0),
        compiler_params=pltpu.CompilerParams(vmem_limit_bytes=vmem_mib << 20),
    )(at, *operands)


def bf16(*shape):
    return jax.ShapeDtypeStruct(shape, jnp.bfloat16)


def f32(*shape):
    return jax.ShapeDtypeStruct(shape, jnp.float32)


def shards(row_emb, col_emb, row_acc, col_acc, counts, live_rows, row_marg, col_marg):
    d, r, c = (lax.axis_index(a) for a in ("dim", "row", "col"))
    core, quad, y = r % 2, (r // 2) % 4, c % 2
    row_emb, col_emb = row_emb[0], col_emb[0]
    col_part = core * 4 + quad
    live_here = live_rows[0, 0] - d * HALF_ROWS
    at = jnp.stack([d, r, c, core, col_part, y, live_here]).astype(jnp.int32)

    def rows_at(block, start, size):
        return lax.dynamic_slice_in_dim(block, start, size, 0)

    col_got = lax.ppermute(rows_at(col_emb, col_part * COL_PART, COL_PART), "dim", DIM_SWAP)
    row_got = lax.ppermute(
        rows_at(row_emb, (1 - d) * HALF_ROWS + y * ROW_PAIR, ROW_PAIR), "dim", DIM_SWAP
    )
    (shared,) = on_device(share_kernel, at, (col_got,), (bf16(4, COL_PART, HALF_D),), 1)
    col_other = lax.all_to_all(shared, "row", 0, 0, axis_index_groups=Z_QUADS)
    (row_got,) = on_device(same_kernel, at, (row_got,), (bf16(ROW_PAIR, HALF_D),), C_SAME)
    there = lax.ppermute(row_got, "col", Y_SWAP)
    col_other = lax.all_gather(col_other, "row", tiled=True, axis_index_groups=CORE_PAIRS)
    col_other = col_other.reshape(SIDE, HALF_D)

    terms = (bf16(HALF_ROWS, WIDTH),) * 3 + (bf16(ROW_PART, WIDTH), bf16(COL_PART, WIDTH))
    col_sum = pltpu.VMEM((SIDE, WIDTH), jnp.float32)
    for step in range(STEPS):
        last = step == STEPS - 1
        if step == 0:
            kept, given, row_term, row_was, col_was, weight, target = on_device(
                first_tile_kernel,
                at,
                (row_emb, row_got, there, col_emb, col_other, counts[0, 0], row_marg, col_marg),
                terms + (f32(HALF_ROWS, SIDE),) * 2,
                3,
                8,
                [col_sum, pltpu.VMEM((HALF_ROWS, WIDTH), jnp.bfloat16), pltpu.VMEM((SIDE, WIDTH), jnp.bfloat16)],
            )
        else:
            kept, given, row_term, row_was, col_was = on_device(
                tile_terms,
                at,
                (rows, cols, weight, target),
                terms,
                3,
                8,
                [col_sum],
            )

        pair = lax.all_gather(given, "row", axis_index_groups=CORE_PAIRS)
        (half,) = on_device(half_kernel, at, (kept, pair), (bf16(4, COL_PART, WIDTH),), 1)
        parts = lax.all_to_all(half, "row", 0, 0, axis_index_groups=Z_QUADS)
        (near,) = on_device(near_kernel, at, (parts,), (bf16(COL_PART, WIDTH),), 1)
        row_term, near = lax.optimization_barrier((row_term, near))
        far = lax.ppermute(near, ("row", "dim"), FAR_Z)

        row_parts = lax.all_to_all(row_term.reshape(N_COL, ROW_PART, WIDTH), "col", 0, 0)
        (near,) = on_device(pair_kernel, at, (near, far), (bf16(COL_PART, WIDTH),), C_PAIR)
        far = lax.ppermute(near, "dim", DIM_SWAP)
        if not last:
            rows, row_acc = on_device(
                row_kernel,
                at,
                (row_parts, row_acc, row_was),
                (bf16(N_COL, ROW_PART, WIDTH), f32(ROW_PART, 1)),
                C_ROW,
            )
            rows = lax.all_to_all(rows, "col", 0, 0).reshape(HALF_ROWS, WIDTH)
            cols, col_acc = on_device(
                col_kernel,
                at,
                (near, far, col_acc, col_was),
                (bf16(COL_PART, WIDTH), f32(COL_PART, 1)),
                C_COL,
            )
            blocks = [cols] + [lax.ppermute(cols, "row", swap) for swap in IN_QUAD]
            rows, *blocks = lax.optimization_barrier((rows, *blocks))
            (cols,) = on_device(quad_kernel, at, blocks, (bf16(4, COL_PART, WIDTH),), C_QUAD)
            cols = lax.all_gather(cols, "row", tiled=True, axis_index_groups=CORE_PAIRS)
            cols = cols.reshape(SIDE, WIDTH)
            continue

        kept, sent = on_device(
            row_last_kernel,
            at,
            (row_parts, row_acc, row_was),
            (bf16(ROW_PART, WIDTH), bf16(ROW_PART, WIDTH)),
            C_ROW_LAST,
        )
        rows_far = lax.ppermute(sent, "dim", DIM_SWAP)
        (cols,) = on_device(
            col_last_kernel, at, (near, far, col_acc, col_was), (bf16(COL_PART, WIDTH),), C_COL_LAST
        )
        blocks = [cols] + [lax.ppermute(cols, "row", swap) for swap in IN_QUAD]
        (rows,) = on_device(
            pack_kernel, at, (kept, rows_far), (bf16(N_COL, ROW_PART, WIDTH + HALF_D),), C_PACK
        )
        rows = lax.all_to_all(rows, "col", 0, 0)
        (cols,) = on_device(quad_kernel, at, blocks, (bf16(4, COL_PART, WIDTH),), C_QUAD)
        cols = lax.all_gather(cols, "row", tiled=True, axis_index_groups=CORE_PAIRS)

    shapes = bf16(1, SIDE, HALF_D), f32(1, SIDE)
    cols = on_device(col_out_kernel, at, (cols.reshape(SIDE, WIDTH),), shapes, C_OUT)
    rows, *cols = lax.optimization_barrier((rows, *cols))
    rows = rows.reshape(HALF_ROWS, WIDTH + HALF_D)
    return (*on_device(row_out_kernel, at, (rows,), shapes, 1), *cols)


def solution(mesh):
    return jax.shard_map(
        shards,
        mesh=mesh,
        in_specs=(
            P("row", None, "dim"),
            P("col", None, "dim"),
            P("row", None),
            P("col", None),
            P("row", "col", "dim", None),
            P("row", "col"),
            P(),
            P(),
        ),
        out_specs=(P("row", None, "dim"), P("row", None), P("col", None, "dim"), P("col", None)),
        check_vma=False,
    )
```
